128 devices in a mesh: row: 8 (over x, z_hi), col: 16 (over y, z_lo, core).
Axes of the slice: x: 4, y: 4, z: 4 (z_hi: 2, z_lo: 2; z = z_hi * 2 + z_lo), core: 2. Of those that a mesh axis runs over, the one named last changes fastest.
Arguments:
- tokens: bfloat16 [2048, 6144], P('col', 'row'), may hold values from -7.5 to 7.5
- ln_gain: float32 [6144], P('row'), may hold values from 0.1 to 1.9
- w_qkv: bfloat16 [6144, 3, 6144], P('row', None, 'col'), may hold values from -0.078125 to 0.078125
- w_up: bfloat16 [6144, 24576], P('row', 'col'), may hold values from -0.078125 to 0.078125
- w_out: bfloat16 [6144, 6144], P('col', 'row'), may hold values from -0.078125 to 0.078125
- w_down: bfloat16 [24576, 6144], P('col', 'row'), may hold values from -0.0390625 to 0.0390625
Outputs:
- layer_out: bfloat16 [2048, 6144], P('col', 'row')
The draws below stay inside these ranges and needn't reach their ends.
All inputs are finite; a program needn't handle non-finite values.
Results may differ from the reference program's by a relative error of at most 0.022.
Values may be sent and summed in bfloat16 or wider, within the bound.
A program may use at most 64 MiB of HBM per device.

```python
import math
import jax
import jax.numpy as jnp
from jax import lax

D = 6144
HEADS = 48
HD = 128
FF = 24576
PATCH = 256
IMGS = 8
TOKENS = 2048
N_ROW = 8


def draw_tokens(key, part):
    key = jax.random.fold_in(key, 11)
    key_base, key_cols = jax.random.split(key, 2)
    base = jnp.clip(jax.random.normal(key_base, (TOKENS, D), jnp.float32), -3.0, 3.0)
    rough = jnp.exp(jax.random.uniform(key_cols, (1, D), jnp.float32, math.log(0.55), math.log(1.1)))
    ramp = jnp.exp(jnp.linspace(math.log(0.35), math.log(2.1), D, dtype=jnp.float32))
    column_scale = rough * ramp[None, :]
    return (base * column_scale).astype(jnp.bfloat16)


def levels(own_key, extent, pieces, smallest, high):
    level, own = 1.0, jax.random.fold_in(own_key, 6)
    for dim, shards_of in pieces:
        steps = jnp.exp(jax.random.uniform(jax.random.fold_in(own, dim), (shards_of,), jnp.float32, smallest / len(pieces), high / len(pieces)))
        level = level * jnp.repeat(steps, extent[dim] // shards_of).reshape([-1 if axis == dim else 1 for axis in range(len(extent))])
    return level


def noise(stream_key, shape, scale, limit, pieces=(), held_as=jnp.bfloat16):
    result = jax.random.normal(stream_key, shape, jnp.float32) * scale
    if len(pieces) > 0:
        result = levels(stream_key, shape, pieces, -0.22, 0.18) * result
    return jnp.clip(result, min=-limit, max=limit).astype(held_as)


def setup_inputs(seed: int = 0) -> dict:
    key_of = jax.random.split(jax.random.key(seed), 7)
    tokens = draw_tokens(jax.random.fold_in(key_of[6], 71), 0)
    ln_gain = jnp.clip(1.0 + 0.18 * jax.random.normal(key_of[1], (D,), jnp.float32), 0.1, 1.9)
    w_qkv = noise(key_of[2], (D, 3, D), D ** -0.5, 0.078125, ((0, 8), (2, 16)))
    w_up = noise(key_of[3], (D, FF), D ** -0.5, 0.078125, ((0, 8), (1, 16)))
    w_out = noise(key_of[4], (D, D), D ** -0.5, 0.078125, ((0, 16), (1, 8)))
    w_down = noise(key_of[5], (FF, D), FF ** -0.5, 0.0390625, ((0, 16), (1, 8)))
    return {"tokens": tokens, "ln_gain": ln_gain, "w_qkv": w_qkv, "w_up": w_up, "w_out": w_out, "w_down": w_down}


epsilon = 1e-06

def row_norm(values):
    average = lax.optimization_barrier(jnp.mean(values, axis=-1, keepdims=True))
    square = lax.optimization_barrier(jnp.mean(values * values, axis=-1, keepdims=True))
    return (values - average) * lax.rsqrt(square - average * average + epsilon)

def blocked_product(normed, weight):
    block_width = D // N_ROW

    def add_block(running, block_index):
        offset = (block_index * block_width).astype(jnp.int32)
        lhs_block = lax.dynamic_slice_in_dim(normed, offset, block_width, 1)
        rhs_block = lax.dynamic_slice_in_dim(weight, offset, block_width, 0)
        piece_term = jnp.dot(lhs_block, rhs_block, preferred_element_type=jnp.float32).astype(jnp.bfloat16)
        piece_term = lax.optimization_barrier(piece_term)
        return (running + piece_term.astype(jnp.float32), None)
    start_sum = jnp.zeros((normed.shape[0], weight.shape[1]), jnp.float32)
    running, _ = lax.scan(add_block, start_sum, jnp.arange(N_ROW, dtype=jnp.int32))
    return running

def attend(image_block):
    queries = row_norm(image_block[:, 0]).astype(jnp.bfloat16)
    key_norm = row_norm(image_block[:, 1]).astype(jnp.bfloat16)
    values = image_block[:, 2].astype(jnp.bfloat16)
    scores = jnp.einsum('phe,qhe->hpq', queries.astype(jnp.float32), key_norm.astype(jnp.float32)) * HD ** (-0.5)
    weights = jnp.exp(scores)
    probabilities = (weights / lax.optimization_barrier(jnp.sum(weights, axis=-1, keepdims=True))).astype(jnp.bfloat16)
    attended = jnp.einsum('hpq,qhe->phe', probabilities.astype(jnp.float32), values.astype(jnp.float32))
    return attended.astype(jnp.bfloat16).reshape(PATCH, HEADS * HD)

def reference(tokens, ln_gain, w_qkv, w_up, w_out, w_down):
    normed = (row_norm(tokens.astype(jnp.float32)) * ln_gain).astype(jnp.bfloat16)
    qkv_sum = blocked_product(normed, w_qkv.reshape(D, 3 * D))
    up_sum = blocked_product(normed, w_up)
    image_blocks = qkv_sum.reshape(IMGS, PATCH, 3, HEADS, HD)
    attended = lax.map(attend, image_blocks).reshape(TOKENS, D)
    hidden = jax.nn.gelu(up_sum, approximate=True).astype(jnp.bfloat16)
    branch = jnp.dot(attended, w_out, preferred_element_type=jnp.float32) + jnp.dot(hidden, w_down, preferred_element_type=jnp.float32)
    return (tokens.astype(jnp.float32) + branch).astype(jnp.bfloat16)
```

```python
import jax
import jax.numpy as jnp
from jax import lax
from jax.experimental import pallas as pl
from jax.experimental.pallas import tpu as pltpu
from jax.sharding import PartitionSpec as P

D = 6144
HD = 128
KB = 768
EPS = 1e-06
F32 = jnp.float32
BF16 = jnp.bfloat16
MESH = pl.DeviceIdType.MESH
N_UP = 3
UP_W = 256
N_MSG = 160
N_LOC = 24


def head_norm(v):
    average = jnp.mean(v, axis=-1, keepdims=True)
    square = jnp.mean(v * v, axis=-1, keepdims=True)
    return ((v - average) * lax.rsqrt(square - average * average + EPS)).astype(BF16)


def attend(qkv):
    q = head_norm(qkv[:, 0:HD])
    k = head_norm(qkv[:, HD : 2 * HD])
    v = qkv[:, 2 * HD : 3 * HD].astype(BF16)
    scores = lax.dot_general(q, k, (((1,), (1,)), ((), ())), preferred_element_type=F32) * HD ** (-0.5)
    weights = jnp.exp(scores)
    probabilities = (weights / jnp.sum(weights, axis=-1, keepdims=True)).astype(BF16)
    return jnp.dot(probabilities, v, preferred_element_type=F32).astype(BF16)


class Ring:
    def __init__(self, send, pos, right, left, piece, a_left, a_right, b_left, b_right):
        self.send, self.right, self.left, self.piece = send, right, left, piece
        self.pos = pos
        self.plus, self.minus, self.anti = (pos + 1) % 4, (pos + 3) % 4, (pos + 2) % 4
        self.a_left, self.a_right, self.b_left, self.b_right = a_left, a_right, b_left, b_right

    def first(self):
        self.ma_r = self.send(self.piece(self.anti, 0), self.a_left, self.right)
        self.ma_l = self.send(self.piece(self.anti, 1), self.a_right, self.left)

    def second(self):
        self.mb_r1 = self.send(self.piece(self.plus, 1), self.b_left[1], self.right)
        self.mb_l0 = self.send(self.piece(self.minus, 0), self.b_right[0], self.left)

    def third(self):
        self.ma_r.wait_recv()
        mine = self.piece(self.plus, 0)
        mine[...] = (mine[...].astype(F32) + self.a_left[...].astype(F32)).astype(BF16)
        self.mb_r0 = self.send(mine, self.b_left[0], self.right)
        self.ma_l.wait_recv()
        mine = self.piece(self.minus, 1)
        mine[...] = (mine[...].astype(F32) + self.a_right[...].astype(F32)).astype(BF16)
        self.mb_l1 = self.send(mine, self.b_right[1], self.left)

    def arrive(self):
        for message in (self.mb_r1, self.mb_l0, self.mb_r0, self.mb_l1):
            message.wait_recv()

    def total(self, half):
        return (
            self.piece(self.pos, half)[...].astype(F32)
            + self.b_left[half][...].astype(F32)
            + self.b_right[half][...].astype(F32)
        )


def kernel(
    tok, gain, wq, wu, wo, wd, out,
    X, W1F, W1S, W1U, W2F, W2S, W2U,
    PF, PS, PU, AF, AS, AU, BF, BS, BU, HF, HS, HU,
    acc, OS, OC, YA0, YB0, OZ, ZA0, ZB0, ZA1, ZB1, OY, YA1, YB1,
    stats, send_sem, recv_sem, loc_sem,
):
    row, col = lax.axis_index("row"), lax.axis_index("col")
    x, zh = row // 2, row % 2
    y, zl, c = col // 4, (col // 2) % 2, col % 2
    z = zh * 2 + zl

    def dev(x_, y_, z_, c_):
        return (x_ * 2 + z_ // 2, y_ * 4 + (z_ % 2) * 2 + c_)

    xr, xl = dev((x + 1) % 4, y, z, c), dev((x + 3) % 4, y, z, c)
    yr, yl = dev(x, (y + 1) % 4, z, c), dev(x, (y + 3) % 4, z, c)
    zr, zlft = dev(x, y, (z + 1) % 4, c), dev(x, y, (z + 3) % 4, c)
    zp = dev(x, y, (z + 2) % 4, c)
    sib = dev(x, y, z, 1 - c)
    row_others = [(lax.rem(row + i, 8), col) for i in range(1, 8)]

    barrier = pltpu.get_barrier_semaphore()
    everyone = row_others + [yr, yl, zr, zlft, sib]
    for who in everyone:
        pl.semaphore_signal(barrier, inc=1, device_id=who, device_id_type=MESH)

    used = [0, 0]
    sent = []

    def send(src, dst, who):
        i = used[0]
        used[0] += 1
        copy = pltpu.make_async_remote_copy(
            src_ref=src, dst_ref=dst, send_sem=send_sem.at[i], recv_sem=recv_sem.at[i],
            device_id=who, device_id_type=MESH,
        )
        copy.start()
        sent.append(copy)
        return copy

    def local(src, dst):
        i = used[1]
        used[1] += 1
        copy = pltpu.make_async_copy(src, dst, loc_sem.at[i])
        copy.start()
        return copy

    def part(n, where):
        return pl.ds(pl.multiple_of(where * n, n), n)

    zo = 1 - zh
    own_k = part(KB, zh)

    def w1_full(who):
        return [(wq.at[j, :, part(HD, 2 * who)], W1F.at[own_k, pl.ds(j * HD, HD)]) for j in range(3)]

    w1_shared = [(wq.at[j, :, pl.ds(HD, HD)], W1S.at[own_k, pl.ds(j * HD, HD)]) for j in range(3)]

    def w1_up(who, k):
        start = pl.multiple_of(who * KB + k * UP_W, UP_W)
        return [(wu.at[:, pl.ds(start, UP_W)], W1U.at[k, own_k])]

    def w2_all(who):
        return [
            (wo.at[part(HD, 2 * who)], W2F.at[:, own_k]),
            (wo.at[pl.ds(HD, HD)], W2S.at[:, own_k]),
        ] + [
            (wd.at[pl.ds(pl.multiple_of(who * KB + k * UP_W, UP_W), UP_W)], W2U.at[k, :, own_k])
            for k in range(N_UP)
        ]

    mine_w1 = [[local(*p) for p in w1_full(zh)], [local(*p) for p in w1_shared]]
    mine_w1 += [[local(*p) for p in w1_up(zh, k)] for k in range(N_UP)]
    mine_w2 = [local(*p) for p in w2_all(zh)]

    values = tok[...].astype(F32)
    sums = [jnp.sum(values, axis=-1, keepdims=True), jnp.sum(values * values, axis=-1, keepdims=True)]
    for i, s in enumerate(sums):
        stats[0, 8 * i : 8 * i + 8] = jnp.transpose(jnp.broadcast_to(s, (128, 128)))[0:8]
    pl.semaphore_wait(barrier, len(everyone))
    moments = [send(stats.at[0], stats.at[i + 1], who) for i, who in enumerate(row_others)]
    partner_w1 = [[send(*p, zp) for p in w1_full(zo)]]
    for m in moments:
        m.wait_recv()
    all_sums = jnp.sum(stats[...], axis=0) / D
    average, square = all_sums[0:1], all_sums[8:9]
    scale = lax.rsqrt(square - average * average + EPS)
    average = jnp.transpose(jnp.broadcast_to(average, (128, 128)))[:, 0:1]
    scale = jnp.transpose(jnp.broadcast_to(scale, (128, 128)))[:, 0:1]
    X[y, zl, c, :, own_k] = ((values - average) * scale * gain[...]).astype(BF16)

    own = X.at[y, zl, c, :, own_k]
    z_msgs = {1: send(own, own, zr), 3: send(own, own, zlft), 2: send(own, own, zp)}

    def x_piece(y_, step):
        z_ = (z + step) % 4
        return X.at[y_, z_ % 2, c, :, part(KB, z_ // 2)]

    y_r, y_l = {}, {}
    for step in (0, 3, 1, 2):
        if step:
            z_msgs[{3: 1, 1: 3, 2: 2}[step]].wait_recv()
        y_r[step] = send(x_piece(y, step), x_piece(y, step), yr)
        y_l[step] = send(x_piece(y, step), x_piece(y, step), yl)
    partner_w1.append([send(*p, zp) for p in w1_shared])
    for k in range(N_UP):
        partner_w1.append([send(*p, zp) for p in w1_up(zo, k)])
    core_msgs = [send(X.at[y, :, c], X.at[y, :, c], sib)]
    yp, ym, ya = (y + 1) % 4, (y + 3) % 4, (y + 2) % 4
    fwd = []
    for step in (0, 3):
        y_r[step].wait_recv()
        fwd.append(send(x_piece(ym, step), x_piece(ym, step), yr))
    for step in (1, 2):
        y_l[step].wait_recv()
        fwd.append(send(x_piece(yp, step), x_piece(yp, step), yl))
    for step in (1, 2):
        y_r[step].wait_recv()
    core_msgs.append(send(X.at[ym, :, c], X.at[ym, :, c], sib))
    for step in (0, 3):
        y_l[step].wait_recv()
    core_msgs.append(send(X.at[yp, :, c], X.at[yp, :, c], sib))
    for m in fwd:
        m.wait_recv()
    core_msgs.append(send(X.at[ya, :, c], X.at[ya, :, c], sib))
    for m in core_msgs:
        m.wait_recv()

    def chunk(kind, k=0):
        if kind == "full":
            p, a, b, h, w1, w2, rows = PF, AF, BF, HF, W1F, W2F, 512
        elif kind == "shared":
            p, a, b, h, w1, w2, rows = PS, AS, BS, HS, W1S, W2S, 256
        else:
            p, a, b, h, w1, w2, rows = PU.at[k], AU.at[k], BU.at[k], HU.at[k], W1U.at[k], W2U.at[k], 512
        half = rows // 2

        def piece(i, which):
            return p.at[i, pl.ds(which * half, half)]

        ring = Ring(
            send, x, xr, xl, piece, a.at[0], a.at[1],
            [b.at[0, pl.ds(w * half, half)] for w in range(2)],
            [b.at[1, pl.ds(w * half, half)] for w in range(2)],
        )
        return dict(kind=kind, k=k, p=p, h=h, w1=w1, w2=w2, rows=rows, half=half, ring=ring)

    chunks = [chunk("full"), chunk("shared")] + [chunk("up", k) for k in range(N_UP)]

    def product(ch, d):
        if ch["kind"] == "shared":
            lhs = X[d, zh].reshape(256, 2 * KB)
        else:
            lhs = X[d].reshape(512, 2 * KB)
        ch["p"][d] = jnp.dot(lhs, ch["w1"][...], preferred_element_type=F32).astype(BF16)

    def stage1(ch, index):
        for copy in mine_w1[index]:
            copy.wait()
        for copy in partner_w1[index]:
            copy.wait_recv()
        product(ch, (x + 2) % 4)
        ch["ring"].first()

        def other(i, carry):
            product(ch, (x + 1 + 2 * i + i // 2 * 3) % 4)
            return carry

        lax.fori_loop(0, 3, other, 0)
        ch["ring"].second()

    def stage2(ch):
        ch["ring"].third()

    def stage3(ch):
        ring, h, half = ch["ring"], ch["h"], ch["half"]
        ring.arrive()
        if ch["kind"] == "up":
            for w in range(2):
                h[x, w * half : (w + 1) * half] = jax.nn.gelu(ring.total(w), approximate=True).astype(BF16)
        elif ch["kind"] == "full":
            for w in range(2):
                h[x, w * half : (w + 1) * half] = attend(ring.total(w))
        else:
            h[x] = attend(jnp.concatenate([ring.total(0), ring.total(1)], axis=0))
        ch["g_r"] = send(h.at[x], h.at[x], xr)
        ch["g_l"] = send(h.at[x], h.at[x], xl)

    def stage4(ch):
        h, half = ch["h"], ch["half"]
        ch["g_r"].wait_recv()
        low = h.at[(x + 3) % 4, pl.ds(0, half)]
        ch["f_r"] = send(low, low, xr)
        ch["g_l"].wait_recv()
        high = h.at[(x + 1) % 4, pl.ds(half, half)]
        ch["f_l"] = send(high, high, xl)

    def stage5(ch, first):
        ch["f_r"].wait_recv()
        ch["f_l"].wait_recv()
        h, w2 = ch["h"], ch["w2"]

        def tile(i, carry):
            d, n = i // 3, i % 3
            columns = part(512, n)
            term = jnp.dot(h[d], w2[:, columns], preferred_element_type=F32)
            if ch["kind"] == "shared":
                term = term.reshape(2, 128, 512)
                acc[d, zh, :, :, columns] += term
            else:
                term = term.reshape(2, 2, 128, 512)
                if first:
                    acc[d, :, :, :, columns] = term
                else:
                    acc[d, :, :, :, columns] += term
            return carry

        lax.fori_loop(0, 12, tile, 0)

    n = len(chunks)
    partner_w2 = []
    for t in range(n + 4):
        if t < n:
            stage1(chunks[t], t)
        if t == 2:
            partner_w2 = [send(*p, zp) for p in w2_all(zo)]
        if 0 <= t - 1 < n:
            stage2(chunks[t - 1])
        if 0 <= t - 2 < n:
            stage3(chunks[t - 2])
        if 0 <= t - 3 < n:
            stage4(chunks[t - 3])
        if 0 <= t - 4 < n:
            if t == 4:
                for copy in mine_w2:
                    copy.wait()
                for copy in partner_w2:
                    copy.wait_recv()
            stage5(chunks[t - 4], t == 4)

    def columns_of(path, which):
        return pl.ds(which * KB + path * 384, 384)

    core_out = []
    for path in range(2):

        def cast(i, carry, path=path):
            for which in range(2):
                OS[path, i // 2, i % 2, :, which * 384 : (which + 1) * 384] = acc[
                    i // 2, i % 2, 1 - c, :, columns_of(path, which)
                ].astype(BF16)
            return carry

        lax.fori_loop(0, 8, cast, 0)
        core_out.append(send(OS.at[path], OC.at[path], sib))

    rings = []
    for path in range(2):
        core_out[path].wait_recv()

        def add(i, carry, path=path):
            for which in range(2):
                there = (path, i // 2, i % 2, slice(None), slice(which * 384, (which + 1) * 384))
                OC[there] = (
                    OC[there].astype(F32) + acc[i // 2, i % 2, c, :, columns_of(path, which)]
                ).astype(BF16)
            return carry

        lax.fori_loop(0, 8, add, 0)
        if path == 0:

            def piece0(i, which):
                return OC.at[0, i, which]

            ring = Ring(send, y, yr, yl, piece0, YA0.at[0], YA0.at[1],
                        [YB0.at[0, w] for w in range(2)], [YB0.at[1, w] for w in range(2)])
        else:

            def piece1(i, which):
                return OC.at[1, pl.ds(which * 2, 2), i % 2, :, part(384, i // 2)]

            ring = Ring(send, z, zr, zlft, piece1, ZA1.at[0], ZA1.at[1],
                        [ZB1.at[0, w] for w in range(2)], [ZB1.at[1, w] for w in range(2)])
        ring.first()
        ring.second()
        rings.append(ring)
    for ring in rings:
        ring.third()
    rings[0].arrive()
    for w in range(2):
        OZ[w] = rings[0].total(w).astype(BF16)

    def piece2(i, which):
        return OZ.at[i % 2, pl.ds(which * 64, 64), part(384, i // 2)]

    last0 = Ring(send, z, zr, zlft, piece2, ZA0.at[0], ZA0.at[1],
                 [ZB0.at[0, w] for w in range(2)], [ZB0.at[1, w] for w in range(2)])
    last0.first()
    last0.second()
    rings[1].arrive()
    for w in range(2):
        OY[2 * w : 2 * w + 2] = rings[1].total(w).astype(BF16)

    def piece3(i, which):
        return OY.at[i, pl.ds(which * 64, 64)]

    last1 = Ring(send, y, yr, yl, piece3, YA1.at[0], YA1.at[1],
                 [YB1.at[0, w] for w in range(2)], [YB1.at[1, w] for w in range(2)])
    last1.first()
    last1.second()
    last0.third()
    last1.third()
    for path, last in enumerate((last0, last1)):
        last.arrive()
        for w in range(2):
            rows, columns = slice(64 * w, 64 * w + 64), slice(384 * path, 384 * path + 384)
            out[rows, columns] = (tok[rows, columns].astype(F32) + last.total(w)).astype(BF16)
    for copy in sent:
        copy.wait_send()


def vm(*shape, dtype=BF16):
    return pltpu.VMEM(shape, dtype)


def body(tokens, ln_gain, w_qkv, w_up, w_out, w_down):
    scratch = [
        vm(4, 2, 2, 128, 1536), vm(1536, 384), vm(1536, 384), vm(N_UP, 1536, UP_W),
        vm(128, 1536), vm(128, 1536), vm(N_UP, UP_W, 1536),
        vm(4, 512, 384), vm(4, 256, 384), vm(N_UP, 4, 512, UP_W),
        vm(2, 256, 384), vm(2, 128, 384), vm(N_UP, 2, 256, UP_W),
        vm(2, 512, 384), vm(2, 256, 384), vm(N_UP, 2, 512, UP_W),
        vm(4, 512, 128), vm(4, 256, 128), vm(N_UP, 4, 512, UP_W),
        vm(4, 2, 2, 128, 1536, dtype=F32),
        vm(2, 4, 2, 128, 768), vm(2, 4, 2, 128, 768),
        vm(2, 128, 768), vm(2, 2, 128, 768), vm(2, 128, 768), vm(2, 64, 384), vm(2, 2, 64, 384),
        vm(2, 2, 128, 384), vm(2, 2, 2, 128, 384), vm(4, 128, 384), vm(2, 64, 384), vm(2, 2, 64, 384),
        vm(8, 16, 128, dtype=F32),
        pltpu.SemaphoreType.DMA((N_MSG,)), pltpu.SemaphoreType.DMA((N_MSG,)), pltpu.SemaphoreType.DMA((N_LOC,)),
    ]
    vmem, anywhere = pl.BlockSpec(memory_space=pltpu.VMEM), pl.BlockSpec(memory_space=pl.ANY)
    return pl.pallas_call(
        kernel,
        out_shape=jax.ShapeDtypeStruct((128, KB), BF16),
        in_specs=[vmem, vmem, anywhere, anywhere, anywhere, anywhere],
        out_specs=vmem,
        scratch_shapes=scratch,
        compiler_params=pltpu.CompilerParams(
            collective_id=0, has_side_effects=True, vmem_limit_bytes=62 << 20
        ),
        name="layer",
    )(tokens, ln_gain.reshape(1, KB), jnp.transpose(w_qkv, (1, 0, 2)), w_up, w_out, w_down)


def solution(mesh):
    return jax.shard_map(
        body,
        mesh=mesh,
        in_specs=(
            P("col", "row"),
            P("row"),
            P("row", None, "col"),
            P("row", "col"),
            P("col", "row"),
            P("col", "row"),
        ),
        out_specs=P("col", "row"),
        check_vma=False,
    )
```

```python
import jax
import jax.numpy as jnp
from jax import lax
from jax.experimental import pallas as pl
from jax.experimental.pallas import tpu as pltpu
from jax.sharding import PartitionSpec as P

D = 6144
HD = 128
KB = 768
EPS = 1e-06
F32 = jnp.float32
BF16 = jnp.bfloat16
MESH = pl.DeviceIdType.MESH
N_UP = 3
UP_W = 256
N_MSG = 256
N_LOC = 24


def head_norm(v):
    average = jnp.mean(v, axis=-1, keepdims=True)
    square = jnp.mean(v * v, axis=-1, keepdims=True)
    return ((v - average) * lax.rsqrt(square - average * average + EPS)).astype(BF16)


def attend(qkv):
    q = head_norm(qkv[:, 0:HD])
    k = head_norm(qkv[:, HD : 2 * HD])
    v = qkv[:, 2 * HD : 3 * HD].astype(BF16)
    scores = lax.dot_general(q, k, (((1,), (1,)), ((), ())), preferred_element_type=F32) * HD ** (-0.5)
    weights = jnp.exp(scores)
    probabilities = (weights / jnp.sum(weights, axis=-1, keepdims=True)).astype(BF16)
    return jnp.dot(probabilities, v, preferred_element_type=F32).astype(BF16)


class Ring:
    def __init__(self, send, pos, right, left, piece, a_left, a_right, b_left, b_right):
        self.send, self.right, self.left, self.piece = send, right, left, piece
        self.pos = pos
        self.plus, self.minus, self.anti = (pos + 1) % 4, (pos + 3) % 4, (pos + 2) % 4
        self.a_left, self.a_right, self.b_left, self.b_right = a_left, a_right, b_left, b_right

    def first(self):
        self.ma_r = self.send(self.piece(self.anti, 0), self.a_left, self.right)
        self.ma_l = self.send(self.piece(self.anti, 1), self.a_right, self.left)

    def second(self):
        self.mb_r1 = self.send(self.piece(self.plus, 1), self.b_left[1], self.right)
        self.mb_l0 = self.send(self.piece(self.minus, 0), self.b_right[0], self.left)

    def third(self):
        self.ma_r.wait_recv()
        mine = self.piece(self.plus, 0)
        mine[...] = (mine[...].astype(F32) + self.a_left[...].astype(F32)).astype(BF16)
        self.mb_r0 = self.send(mine, self.b_left[0], self.right)
        self.ma_l.wait_recv()
        mine = self.piece(self.minus, 1)
        mine[...] = (mine[...].astype(F32) + self.a_right[...].astype(F32)).astype(BF16)
        self.mb_l1 = self.send(mine, self.b_right[1], self.left)

    def arrive(self):
        for message in (self.mb_r1, self.mb_l0, self.mb_r0, self.mb_l1):
            message.wait_recv()

    def total(self, half):
        return (
            self.piece(self.pos, half)[...].astype(F32)
            + self.b_left[half][...].astype(F32)
            + self.b_right[half][...].astype(F32)
        )


N_OUT = 6


def kernel(
    tok, gain, wq, wu, wo, wd, out,
    X, W1F, W1S, W1U, W2F, W2S, W2U,
    PF, PS, PU, AF, AS, AU, BF, BS, BU, HF, HS, HU,
    acc, OS, OC, Y0A, Y0B, Z0P, Z0A, Z0B, Z1A, Z1B, Y1P, Y1A, Y1B,
    stats, send_sem, recv_sem, loc_sem,
):
    row, col = lax.axis_index("row"), lax.axis_index("col")
    x, zh = row // 2, row % 2
    y, zl, c = col // 4, (col // 2) % 2, col % 2
    z = zh * 2 + zl

    def dev(x_, y_, z_, c_):
        return (x_ * 2 + z_ // 2, y_ * 4 + (z_ % 2) * 2 + c_)

    xr, xl, xa = dev((x + 1) % 4, y, z, c), dev((x + 3) % 4, y, z, c), dev((x + 2) % 4, y, z, c)
    yr, yl = dev(x, (y + 1) % 4, z, c), dev(x, (y + 3) % 4, z, c)
    zr, zlft = dev(x, y, (z + 1) % 4, c), dev(x, y, (z + 3) % 4, c)
    zp = dev(x, y, (z + 2) % 4, c)
    sib = dev(x, y, z, 1 - c)

    barrier = pltpu.get_barrier_semaphore()
    everyone = [xa, zp, xr, xl, yr, yl, zr, zlft, sib]
    for who in everyone:
        pl.semaphore_signal(barrier, inc=1, device_id=who, device_id_type=MESH)

    used = [0, 0]
    sent = []

    def send(src, dst, who):
        i = used[0]
        used[0] += 1
        copy = pltpu.make_async_remote_copy(
            src_ref=src, dst_ref=dst, send_sem=send_sem.at[i], recv_sem=recv_sem.at[i],
            device_id=who, device_id_type=MESH,
        )
        copy.start()
        sent.append(copy)
        return copy

    def local(src, dst):
        i = used[1]
        used[1] += 1
        copy = pltpu.make_async_copy(src, dst, loc_sem.at[i])
        copy.start()
        return copy

    def part(n, where):
        return pl.ds(pl.multiple_of(where * n, n), n)

    zo = 1 - zh
    own_k = part(KB, zh)

    values = tok[...].astype(F32)
    sums = [jnp.sum(values, axis=-1, keepdims=True), jnp.sum(values * values, axis=-1, keepdims=True)]
    for i, s in enumerate(sums):
        stats[0, 8 * i : 8 * i + 8] = jnp.transpose(jnp.broadcast_to(s, (128, 128)))[0:8]
    pl.semaphore_wait(barrier, len(everyone))
    send(stats.at[0], stats.at[1], zp).wait_recv()
    stats[2] = stats[0] + stats[1]
    moments = [send(stats.at[2], stats.at[3 + i], who) for i, who in enumerate((xr, xl, xa))]

    def w1_full(who):
        return [(wq.at[j, :, part(HD, 2 * who)], W1F.at[own_k, pl.ds(j * HD, HD)]) for j in range(3)]

    w1_shared = [(wq.at[j, :, pl.ds(HD, HD)], W1S.at[own_k, pl.ds(j * HD, HD)]) for j in range(3)]

    def up_part(who, k):
        return pl.ds(pl.multiple_of(who * KB + k * UP_W, UP_W), UP_W)

    def w1_parts(who):
        parts = [[(wu.at[:, up_part(who, k)], W1U.at[k, own_k])] for k in range(N_UP)]
        return parts + [w1_full(who), w1_shared]

    def w2_parts(who):
        parts = [[(wd.at[up_part(who, k)], W2U.at[k, :, own_k])] for k in range(N_UP)]
        return parts + [
            [(wo.at[part(HD, 2 * who)], W2F.at[:, own_k])],
            [(wo.at[pl.ds(HD, HD)], W2S.at[:, own_k])],
        ]

    mine_w1 = [[local(*p) for p in ps] for ps in w1_parts(zh)]
    mine_w2 = [[local(*p) for p in ps] for ps in w2_parts(zh)]
    for m in moments:
        m.wait_recv()
    all_sums = (stats[2] + stats[3] + stats[4] + stats[5]) / D
    average, square = all_sums[0:1], all_sums[8:9]
    scale = lax.rsqrt(square - average * average + EPS)
    average = jnp.transpose(jnp.broadcast_to(average, (128, 128)))[:, 0:1]
    scale = jnp.transpose(jnp.broadcast_to(scale, (128, 128)))[:, 0:1]
    X[y, zl, c, :, own_k] = ((values - average) * scale * gain[...].reshape(1, KB)).astype(BF16)

    own = X.at[y, zl, c, :, own_k]
    z_msgs = {3: send(own, own, zr), 1: send(own, own, zlft), 2: send(own, own, zp)}
    partner_w1 = [[send(*p, zp) for p in ps] for ps in w1_parts(zo)]
    partner_w2 = [[send(*p, zp) for p in ps] for ps in w2_parts(zo)]

    def x_piece(y_, step):
        z_ = (z + step) % 4
        return X.at[y_, z_ % 2, c, :, part(KB, z_ // 2)]

    yp, ym, ya = (y + 1) % 4, (y + 3) % 4, (y + 2) % 4
    y_r, y_l, core_msgs, fwd = {}, {}, {}, []
    for step in (0, 3, 1, 2):
        if step:
            z_msgs[step].wait_recv()
        y_r[step] = send(x_piece(y, step), x_piece(y, step), yr)
        y_l[step] = send(x_piece(y, step), x_piece(y, step), yl)
    core_msgs[0] = send(X.at[y, :, c], X.at[y, :, c], sib)

    def gather_forward():
        for step in (0, 3):
            y_r[step].wait_recv()
            fwd.append(send(x_piece(ym, step), x_piece(ym, step), yr))
        for step in (1, 2):
            y_l[step].wait_recv()
            fwd.append(send(x_piece(yp, step), x_piece(yp, step), yl))

    def gather_near():
        for step in (1, 2):
            y_r[step].wait_recv()
        core_msgs[2] = send(X.at[ym, :, c], X.at[ym, :, c], sib)
        for step in (0, 3):
            y_l[step].wait_recv()
        core_msgs[1] = send(X.at[yp, :, c], X.at[yp, :, c], sib)
        for i in (2, 1):
            core_msgs[i].wait_recv()

    def gather_far():
        for m in fwd:
            m.wait_recv()
        core_msgs[3] = send(X.at[ya, :, c], X.at[ya, :, c], sib)
        core_msgs[3].wait_recv()

    def unit(kind, k, group=None):
        if kind == "full":
            p, a, b, h = PF, AF, BF, HF
        elif kind == "shared":
            p, a, b, h = PS, AS, BS, HS
        else:
            p, a, b, h = PU.at[k], AU.at[k], BU.at[k], HU.at[k]
        rows = {"full": 256, "shared": 128}.get(kind)
        blocks = None

        def at(half=None):
            if rows:
                return () if half is None else (pl.ds(rows * half, rows),)
            if group is None:
                return () if half is None else (pl.ds(2 * half, 2),)
            if group == 1:
                return (pl.ds(1, 2),) if half is None else (1 + half,)
            return (blocks[0],) if half is None else (blocks[0], pl.ds(64 * half, 64))

        if kind == "up":
            blocks = {None: (0, 1, 2, 3), 0: (0,), 1: (1, 2), 2: (3,)}[group]
        if rows or group is None:
            a_l, a_r = a.at[0], a.at[1]
        elif group == 1:
            a_l, a_r = a.at[0, 1], a.at[1, 1]
        else:
            a_l, a_r = (a.at[side, 0, pl.ds(32 * group, 64)] for side in range(2))
        ring = Ring(
            send, x, xr, xl, lambda i, half: p.at[(i, *at(half))], a_l, a_r,
            [b.at[(0, *at(half))] for half in range(2)], [b.at[(1, *at(half))] for half in range(2)],
        )
        return dict(kind=kind, k=k, p=p, h=h, at=at, blocks=blocks, ring=ring)

    def columns_ready(parts, partner, k):
        for copy in parts[k]:
            copy.wait()
        for copy in partner[k]:
            copy.wait_recv()
        parts[k], partner[k] = [], []

    def produce(u):
        columns_ready(mine_w1, partner_w1, u["k"])
        kind, ring, p = u["kind"], u["ring"], u["p"]
        if kind == "up":
            w1, blocks = W1U.at[u["k"]], u["blocks"]

            def one(i, carry):
                beta = blocks[0] + i
                b = (y + beta + beta // 2 - 2 * (beta // 3)) % 4
                term = jnp.dot(X[b].reshape(512, 2 * KB), w1[...], preferred_element_type=F32)
                p[:, beta] = term.reshape(4, 128, UP_W).astype(BF16)
                return carry

            lax.fori_loop(0, len(blocks), one, 0)
            ring.first()
            ring.second()
            return

        def place(d):
            if kind == "shared":
                lhs, w1 = X[d, zh].reshape(256, 2 * KB), W1S
            else:
                lhs, w1 = X[d].reshape(512, 2 * KB), W1F
            p[d] = jnp.dot(lhs, w1[...], preferred_element_type=F32).astype(BF16)

        place((x + 2) % 4)
        ring.first()

        def other(i, carry):
            place((x + 1 + 2 * i + i // 2 * 3) % 4)
            return carry

        lax.fori_loop(0, 3, other, 0)
        ring.second()

    def combine(u):
        u["ring"].third()

    def activate(u):
        kind, ring, h, at = u["kind"], u["ring"], u["h"], u["at"]
        ring.arrive()
        if kind == "up":
            for half in range(2):
                h[(x, *at(half))] = jax.nn.gelu(ring.total(half), approximate=True).astype(BF16)
        elif kind == "full":
            for half in range(2):
                h[(x, *at(half))] = attend(ring.total(half))
        else:
            h[x] = attend(jnp.concatenate([ring.total(0), ring.total(1)], axis=0))
        mine = h.at[(x, *at())]
        u["g_r"] = send(mine, mine, xr)
        u["g_l"] = send(mine, mine, xl)

    def forward(u):
        h, at = u["h"], u["at"]
        u["g_r"].wait_recv()
        low = h.at[((x + 3) % 4, *at(0))]
        u["f_r"] = send(low, low, xr)
        u["g_l"].wait_recv()
        high = h.at[((x + 1) % 4, *at(1))]
        u["f_l"] = send(high, high, xl)

    def landed(*units):
        for u in units:
            u["f_r"].wait_recv()
            u["f_l"].wait_recv()

    def out_columns(w2, s):
        return jnp.concatenate([w2[:, part(128, s)], w2[:, pl.ds(pl.multiple_of(KB + s * 128, 128), 128)]], axis=1)

    def finish_up(k):
        columns_ready(mine_w2, partner_w2, k)
        h, w2 = HU.at[k], W2U.at[k]

        def tile(i, carry):
            beta, s = i // N_OUT, i % N_OUT
            b = (y + beta + beta // 2 - 2 * (beta // 3)) % 4
            term = jnp.dot(h[:, beta].reshape(512, UP_W), out_columns(w2, s), preferred_element_type=F32)
            term = term.reshape(2, 2, 128, 256)
            if k == 0:
                acc[s, b] = term
            else:
                acc[s, b] += term
            return carry

        lax.fori_loop(0, 4 * N_OUT, tile, 0)

    def finish_full():
        columns_ready(mine_w2, partner_w2, 3)

        def tile(i, carry):
            d, s = i // N_OUT, i % N_OUT
            term = jnp.dot(HF[d], out_columns(W2F, s), preferred_element_type=F32)
            acc[s, d] += term.reshape(2, 2, 128, 256)
            return carry

        lax.fori_loop(0, 4 * N_OUT, tile, 0)

    near = [unit("up", k, 0) for k in range(2)]
    middle = [unit("up", k, 1) for k in range(2)]
    far = [unit("up", k, 2) for k in range(2)]
    whole = unit("up", 2)
    full, shared = unit("full", 3), unit("shared", 4)

    core_msgs[0].wait_recv()
    produce(near[0])
    combine(near[0])
    gather_forward()
    produce(near[1])
    activate(near[0])
    combine(near[1])
    gather_near()
    produce(middle[0])
    produce(middle[1])
    forward(near[0])
    activate(near[1])
    combine(middle[0])
    combine(middle[1])
    gather_far()
    produce(far[0])
    produce(far[1])
    forward(near[1])
    activate(middle[0])
    combine(far[0])
    activate(middle[1])
    combine(far[1])
    produce(whole)
    activate(far[0])
    activate(far[1])
    forward(middle[0])
    forward(middle[1])
    combine(whole)
    produce(full)
    forward(far[0])
    forward(far[1])
    activate(whole)
    combine(full)
    produce(shared)
    forward(whole)
    activate(full)
    combine(shared)
    landed(near[0], middle[0], far[0])
    finish_up(0)
    forward(full)
    activate(shared)
    landed(near[1], middle[1], far[1])
    finish_up(1)
    forward(shared)
    landed(whole)
    finish_up(2)
    landed(full)
    finish_full()
    landed(shared)
    columns_ready(mine_w2, partner_w2, 4)

    def out_core(s):
        columns = out_columns(W2S, s)

        def one(d, carry):
            term = jnp.dot(HS[d], columns, preferred_element_type=F32)
            acc[s, d, zh] += term.reshape(2, 128, 256)
            OS[s, d] = acc[s, d, :, 1 - c].astype(BF16)
            return carry

        lax.fori_loop(0, 4, one, 0)
        return send(OS.at[s], OC.at[s], sib)

    def out_first(s, message):
        message.wait_recv()

        def one(d, carry):
            OC[s, d] = (OC[s, d].astype(F32) + acc[s, d, :, c]).astype(BF16)
            return carry

        lax.fori_loop(0, 4, one, 0)
        if s < 3:
            ring = Ring(
                send, y, yr, yl, lambda i, half: OC.at[s, i, half], Y0A.at[s, 0], Y0A.at[s, 1],
                [Y0B.at[s, 0, half] for half in range(2)], [Y0B.at[s, 1, half] for half in range(2)],
            )
        else:
            ring = Ring(
                send, z, zr, zlft,
                lambda i, half: OC.at[s, pl.ds(2 * half, 2), i % 2, :, part(128, i // 2)],
                Z1A.at[s - 3, 0], Z1A.at[s - 3, 1],
                [Z1B.at[s - 3, 0, half] for half in range(2)], [Z1B.at[s - 3, 1, half] for half in range(2)],
            )
        ring.first()
        ring.second()
        return ring

    def out_second(s, before):
        before.arrive()
        if s < 3:
            for half in range(2):
                Z0P[s, half] = before.total(half).astype(BF16)
            ring = Ring(
                send, z, zr, zlft,
                lambda i, half: Z0P.at[s, i % 2, pl.ds(64 * half, 64), part(128, i // 2)],
                Z0A.at[s, 0], Z0A.at[s, 1],
                [Z0B.at[s, 0, half] for half in range(2)], [Z0B.at[s, 1, half] for half in range(2)],
            )
        else:
            j = s - 3
            for half in range(2):
                Y1P[j, 2 * half : 2 * half + 2] = before.total(half).astype(BF16)
            ring = Ring(
                send, y, yr, yl, lambda i, half: Y1P.at[j, i, pl.ds(64 * half, 64)],
                Y1A.at[j, 0], Y1A.at[j, 1],
                [Y1B.at[j, 0, half] for half in range(2)], [Y1B.at[j, 1, half] for half in range(2)],
            )
        ring.first()
        ring.second()
        return ring

    def out_last(s, ring):
        ring.arrive()
        for half in range(2):
            rows, columns = slice(64 * half, 64 * half + 64), slice(128 * s, 128 * s + 128)
            out[rows, columns] = (tok[rows, columns].astype(F32) + ring.total(half)).astype(BF16)

    sequence = (0, 3, 1, 4, 2, 5)
    core, one, two = {}, {}, {}
    for t in range(N_OUT + 8):
        if t < N_OUT:
            core[t] = out_core(sequence[t])
        if 0 <= t - 1 < N_OUT:
            one[t - 1] = out_first(sequence[t - 1], core[t - 1])
        if 0 <= t - 3 < N_OUT:
            one[t - 3].third()
        if 0 <= t - 5 < N_OUT:
            two[t - 5] = out_second(sequence[t - 5], one[t - 5])
        if 0 <= t - 6 < N_OUT:
            two[t - 6].third()
        if 0 <= t - 8 < N_OUT:
            out_last(sequence[t - 8], two[t - 8])
    for copy in sent:
        copy.wait_send()


def vm(*shape, dtype=BF16):
    return pltpu.VMEM(shape, dtype)


def body(tokens, ln_gain, w_qkv, w_up, w_out, w_down):
    scratch = [
        vm(4, 2, 2, 128, 1536), vm(1536, 384), vm(1536, 384), vm(N_UP, 1536, UP_W),
        vm(128, 1536), vm(128, 1536), vm(N_UP, UP_W, 1536),
        vm(4, 512, 384), vm(4, 256, 384), vm(N_UP, 4, 4, 128, UP_W),
        vm(2, 256, 384), vm(2, 128, 384), vm(N_UP, 2, 2, 128, UP_W),
        vm(2, 512, 384), vm(2, 256, 384), vm(N_UP, 2, 4, 128, UP_W),
        vm(4, 512, 128), vm(4, 256, 128), vm(N_UP, 4, 4, 128, UP_W),
        vm(N_OUT, 4, 2, 2, 128, 256, dtype=F32), vm(N_OUT, 4, 2, 128, 256), vm(N_OUT, 4, 2, 128, 256),
        vm(3, 2, 128, 256), vm(3, 2, 2, 128, 256), vm(3, 2, 128, 256), vm(3, 2, 64, 128), vm(3, 2, 2, 64, 128),
        vm(3, 2, 2, 128, 128), vm(3, 2, 2, 2, 128, 128), vm(3, 4, 128, 128), vm(3, 2, 64, 128), vm(3, 2, 2, 64, 128),
        vm(8, 16, 128, dtype=F32),
        pltpu.SemaphoreType.DMA((N_MSG,)), pltpu.SemaphoreType.DMA((N_MSG,)), pltpu.SemaphoreType.DMA((N_LOC,)),
    ]
    vmem, anywhere = pl.BlockSpec(memory_space=pltpu.VMEM), pl.BlockSpec(memory_space=pl.ANY)
    return pl.pallas_call(
        kernel,
        out_shape=jax.ShapeDtypeStruct((128, KB), BF16),
        in_specs=[vmem, vmem, anywhere, anywhere, anywhere, anywhere],
        out_specs=vmem,
        scratch_shapes=scratch,
        compiler_params=pltpu.CompilerParams(
            collective_id=0, has_side_effects=True, vmem_limit_bytes=62 << 20
        ),
        name="layer",
    )(tokens, ln_gain, jnp.transpose(w_qkv, (1, 0, 2)), w_up, w_out, w_down)


def solution(mesh):
    return jax.shard_map(
        body,
        mesh=mesh,
        in_specs=(
            P("col", "row"),
            P("row"),
            P("row", None, "col"),
            P("row", "col"),
            P("col", "row"),
            P("col", "row"),
        ),
        out_specs=P("col", "row"),
        check_vma=False,
    )
```

```python
import jax
import jax.numpy as jnp
from jax import lax
from jax.experimental import pallas as pl
from jax.experimental.pallas import tpu as pltpu
from jax.sharding import PartitionSpec as P

D = 6144
HD = 128
KB = 768
PATCH = 256
EPS = 1e-06
F32 = jnp.float32
BF16 = jnp.bfloat16
MESH = pl.DeviceIdType.MESH
N_UP = 3
UP_W = 256
N_MSG = 256
N_LOC = 24


def head_norm(v):
    average = jnp.mean(v, axis=-1, keepdims=True)
    square = jnp.mean(v * v, axis=-1, keepdims=True)
    return ((v - average) * lax.rsqrt(square - average * average + EPS)).astype(BF16)


def attend(qkv):
    q = head_norm(qkv[:, 0:HD])
    k = head_norm(qkv[:, HD : 2 * HD])
    v = qkv[:, 2 * HD : 3 * HD].astype(BF16)
    scores = lax.dot_general(q, k, (((1,), (1,)), ((), ())), preferred_element_type=F32) * HD ** (-0.5)
    weights = jnp.exp(scores)
    probabilities = (weights / jnp.sum(weights, axis=-1, keepdims=True)).astype(BF16)
    return jnp.dot(probabilities, v, preferred_element_type=F32).astype(BF16)


class Ring:
    def __init__(self, send, pos, right, left, piece, a_left, a_right, b_left, b_right):
        self.send, self.right, self.left, self.piece = send, right, left, piece
        self.pos = pos
        self.plus, self.minus, self.anti = (pos + 1) % 4, (pos + 3) % 4, (pos + 2) % 4
        self.a_left, self.a_right, self.b_left, self.b_right = a_left, a_right, b_left, b_right

    def first(self):
        self.ma_r = self.send(self.piece(self.anti, 0), self.a_left, self.right)
        self.ma_l = self.send(self.piece(self.anti, 1), self.a_right, self.left)

    def second(self):
        self.mb_r1 = self.send(self.piece(self.plus, 1), self.b_left[1], self.right)
        self.mb_l0 = self.send(self.piece(self.minus, 0), self.b_right[0], self.left)

    def third(self):
        self.ma_r.wait_recv()
        mine = self.piece(self.plus, 0)
        mine[...] = (mine[...].astype(F32) + self.a_left[...].astype(F32)).astype(BF16)
        self.mb_r0 = self.send(mine, self.b_left[0], self.right)
        self.ma_l.wait_recv()
        mine = self.piece(self.minus, 1)
        mine[...] = (mine[...].astype(F32) + self.a_right[...].astype(F32)).astype(BF16)
        self.mb_l1 = self.send(mine, self.b_right[1], self.left)

    def arrive(self):
        for message in (self.mb_r1, self.mb_l0, self.mb_r0, self.mb_l1):
            message.wait_recv()

    def total(self, half):
        return (
            self.piece(self.pos, half)[...].astype(F32)
            + self.b_left[half][...].astype(F32)
            + self.b_right[half][...].astype(F32)
        )


N_OUT = 6


def kernel(
    tok, gain, wq, wu, wo, wd, out,
    X, W1F, W1S, W1U, W2,
    PF, PS, PU, AF, AS, AU, BF, BS, BU, HF, HS, HU,
    acc, OS, OC, Y0A, Y0B, Z0P, Z0A, Z0B, Z1A, Z1B, Y1P, Y1A, Y1B,
    stats, send_sem, recv_sem, loc_sem,
):
    row, col = lax.axis_index("row"), lax.axis_index("col")
    x, zh = row // 2, row % 2
    y, zl, c = col // 4, (col // 2) % 2, col % 2
    z = zh * 2 + zl

    def dev(x_, y_, z_, c_):
        return (x_ * 2 + z_ // 2, y_ * 4 + (z_ % 2) * 2 + c_)

    xr, xl = dev((x + 1) % 4, y, z, c), dev((x + 3) % 4, y, z, c)
    yr, yl = dev(x, (y + 1) % 4, z, c), dev(x, (y + 3) % 4, z, c)
    zr, zlft = dev(x, y, (z + 1) % 4, c), dev(x, y, (z + 3) % 4, c)
    zp = dev(x, y, (z + 2) % 4, c)
    sib = dev(x, y, z, 1 - c)
    zo = 1 - zh

    barrier = pltpu.get_barrier_semaphore()
    row_others = [(lax.rem(row + i, 8), col) for i in range(1, 8)]
    everyone = row_others + [yr, yl, zr, zlft, sib]
    for who in everyone:
        pl.semaphore_signal(barrier, inc=1, device_id=who, device_id_type=MESH)

    used = [0, 0]
    sent = []

    def send(src, dst, who):
        i = used[0]
        used[0] += 1
        copy = pltpu.make_async_remote_copy(
            src_ref=src, dst_ref=dst, send_sem=send_sem.at[i], recv_sem=recv_sem.at[i],
            device_id=who, device_id_type=MESH,
        )
        copy.start()
        sent.append(copy)
        return copy

    def local(src, dst):
        i = used[1]
        used[1] += 1
        copy = pltpu.make_async_copy(src, dst, loc_sem.at[i])
        copy.start()
        return copy

    def part(n, where):
        return pl.ds(pl.multiple_of(where * n, n), n)

    for d in range(4):
        HS[d, zo] = jnp.zeros((PATCH, HD), BF16)

    own_k = part(KB, zh)

    values = tok[...].astype(F32)
    sums = [jnp.sum(values, axis=-1, keepdims=True), jnp.sum(values * values, axis=-1, keepdims=True)]
    for i, s in enumerate(sums):
        stats[0, 8 * i : 8 * i + 8] = jnp.transpose(jnp.broadcast_to(s, (128, 128)))[0:8]
    pl.semaphore_wait(barrier, len(everyone))
    moments = [send(stats.at[0], stats.at[i + 1], who) for i, who in enumerate(row_others)]

    def w1_full(who):
        return [(wq.at[j, :, part(HD, 2 * who)], W1F.at[own_k, pl.ds(j * HD, HD)]) for j in range(3)]

    w1_shared = [(wq.at[j, :, pl.ds(HD, HD)], W1S.at[own_k, pl.ds(j * HD, HD)]) for j in range(3)]

    def up_part(who, k):
        return pl.ds(pl.multiple_of(who * KB + k * UP_W, UP_W), UP_W)

    def w1_parts(who):
        parts = [[(wu.at[:, up_part(who, k)], W1U.at[k, own_k])] for k in range(N_UP)]
        return parts + [w1_full(who), w1_shared]

    def w2_parts(who):
        return [
            [(wd.at[pl.ds(pl.multiple_of(who * KB, KB), 512)], W2.at[pl.ds(0, 512), own_k])],
            [
                (wd.at[up_part(who, 2)], W2.at[pl.ds(512, UP_W), own_k]),
                (wo.at[part(HD, 2 * who)], W2.at[pl.ds(768, HD), own_k]),
                (wo.at[pl.ds(HD, HD)], W2.at[pl.ds(896, HD), own_k]),
            ],
        ]

    partner_w1 = [[send(*p, zp) for p in ps] for ps in w1_parts(zo)[:1]]
    mine_w1 = [[local(*p) for p in ps] for ps in w1_parts(zh)]
    mine_w2 = [[local(*p) for p in ps] for ps in w2_parts(zh)]
    for m in moments:
        m.wait_recv()
    all_sums = jnp.sum(stats[...], axis=0) / D
    average, square = all_sums[0:1], all_sums[8:9]
    scale = lax.rsqrt(square - average * average + EPS)
    average = jnp.transpose(jnp.broadcast_to(average, (128, 128)))[:, 0:1]
    scale = jnp.transpose(jnp.broadcast_to(scale, (128, 128)))[:, 0:1]
    X[y, zl, c, :, own_k] = ((values - average) * scale * gain[...].reshape(1, KB)).astype(BF16)

    own = X.at[y, zl, c, :, own_k]
    z_msgs = {3: send(own, own, zr), 1: send(own, own, zlft), 2: send(own, own, zp)}
    partner_w1 += [[send(*p, zp) for p in ps] for ps in w1_parts(zo)[1:]]
    partner_w2 = [[send(*p, zp) for p in ps] for ps in w2_parts(zo)]

    def x_piece(y_, step):
        z_ = (z + step) % 4
        return X.at[y_, z_ % 2, c, :, part(KB, z_ // 2)]

    yp, ym, ya = (y + 1) % 4, (y + 3) % 4, (y + 2) % 4
    y_r, y_l, core_msgs, fwd = {}, {}, {}, []
    for step in (0, 3, 1, 2):
        if step:
            z_msgs[step].wait_recv()
        y_r[step] = send(x_piece(y, step), x_piece(y, step), yr)
        y_l[step] = send(x_piece(y, step), x_piece(y, step), yl)
    core_msgs[0] = send(X.at[y, :, c], X.at[y, :, c], sib)

    def gather_forward():
        for step in (0, 3):
            y_r[step].wait_recv()
            fwd.append(send(x_piece(ym, step), x_piece(ym, step), yr))
        for step in (1, 2):
            y_l[step].wait_recv()
            fwd.append(send(x_piece(yp, step), x_piece(yp, step), yl))

    def gather_near():
        for step in (1, 2):
            y_r[step].wait_recv()
        core_msgs[2] = send(X.at[ym, :, c], X.at[ym, :, c], sib)
        for step in (0, 3):
            y_l[step].wait_recv()
        core_msgs[1] = send(X.at[yp, :, c], X.at[yp, :, c], sib)
        for i in (2, 1):
            core_msgs[i].wait_recv()

    def gather_far():
        for m in fwd:
            m.wait_recv()
        core_msgs[3] = send(X.at[ya, :, c], X.at[ya, :, c], sib)
        core_msgs[3].wait_recv()

    def unit(kind, k, group=None):
        if kind == "full":
            p, a, b, h = PF, AF, BF, HF
        elif kind == "shared":
            p, a, b, h = PS, AS, BS, HS
        else:
            p, a, b, h = PU.at[k], AU.at[k], BU.at[k], HU.at[k]
        rows = {"full": 256, "shared": 128}.get(kind)
        base = (zh,) if kind == "shared" else ()
        blocks = None

        def at(half=None):
            if rows:
                return () if half is None else (pl.ds(rows * half, rows),)
            if group is None:
                return () if half is None else (pl.ds(2 * half, 2),)
            if group == 1:
                return (pl.ds(1, 2),) if half is None else (1 + half,)
            return (blocks[0],) if half is None else (blocks[0], pl.ds(64 * half, 64))

        if kind == "up":
            blocks = {None: (0, 1, 2, 3), 0: (0,), 1: (1, 2), 2: (3,)}[group]
        if rows or group is None:
            a_l, a_r = a.at[0], a.at[1]
        elif group == 1:
            a_l, a_r = a.at[0, 1], a.at[1, 1]
        else:
            a_l, a_r = (a.at[side, 0, pl.ds(32 * group, 64)] for side in range(2))
        ring = Ring(
            send, x, xr, xl, lambda i, half: p.at[(i, *at(half))], a_l, a_r,
            [b.at[(0, *at(half))] for half in range(2)], [b.at[(1, *at(half))] for half in range(2)],
        )
        return dict(kind=kind, k=k, p=p, h=h, at=at, base=base, blocks=blocks, ring=ring)

    def columns_ready(parts, partner, k):
        for copy in parts[k]:
            copy.wait()
        for copy in partner[k]:
            copy.wait_recv()
        parts[k], partner[k] = [], []

    def produce(u):
        columns_ready(mine_w1, partner_w1, u["k"])
        kind, ring, p = u["kind"], u["ring"], u["p"]
        if kind == "up":
            w1, blocks = W1U.at[u["k"]], u["blocks"]

            def one(i, carry):
                beta = blocks[0] + i
                b = block_at(beta)
                term = jnp.dot(X[b].reshape(512, 2 * KB), w1[...], preferred_element_type=F32)
                p[:, beta] = term.reshape(4, 128, UP_W).astype(BF16)
                return carry

            lax.fori_loop(0, len(blocks), one, 0)
            ring.first()
            ring.second()
            return

        def place(d):
            if kind == "shared":
                lhs, w1 = X[d, zh].reshape(256, 2 * KB), W1S
            else:
                lhs, w1 = X[d].reshape(512, 2 * KB), W1F
            p[d] = jnp.dot(lhs, w1[...], preferred_element_type=F32).astype(BF16)

        place((x + 2) % 4)
        ring.first()

        def other(i, carry):
            place((x + 1 + 2 * i + i // 2 * 3) % 4)
            return carry

        lax.fori_loop(0, 3, other, 0)
        ring.second()

    def combine(u):
        u["ring"].third()

    def activate(u):
        kind, ring, h, at = u["kind"], u["ring"], u["h"], u["at"]
        ring.arrive()
        if kind == "up":
            for half in range(2):
                h[(x, *at(half))] = jax.nn.gelu(ring.total(half), approximate=True).astype(BF16)
        elif kind == "full":
            for half in range(2):
                h[(x, *at(half))] = attend(ring.total(half))
        else:
            h[x, zh] = attend(jnp.concatenate([ring.total(0), ring.total(1)], axis=0))
        mine = h.at[(x, *u["base"], *at())]
        u["g_r"] = send(mine, mine, xr)
        u["g_l"] = send(mine, mine, xl)

    def forward(u):
        h, at = u["h"], u["at"]
        u["g_r"].wait_recv()
        low = h.at[((x + 3) % 4, *u["base"], *at(0))]
        u["f_r"] = send(low, low, xr)
        u["g_l"].wait_recv()
        high = h.at[((x + 1) % 4, *u["base"], *at(1))]
        u["f_l"] = send(high, high, xl)

    def landed(*units):
        for u in units:
            u["f_r"].wait_recv()
            u["f_l"].wait_recv()

    def out_columns(first, s):
        rows = pl.ds(first, 512)
        left, right = part(128, s), pl.ds(pl.multiple_of(KB + s * 128, 128), 128)
        return jnp.concatenate([W2[rows, left], W2[rows, right]], axis=1)

    def block_at(beta):
        return (y + beta + beta // 2 - 2 * (beta // 3)) % 4

    def second_product():
        columns_ready(mine_w2, partner_w2, 0)

        def tile(i, carry):
            beta, s = i // N_OUT, i % N_OUT
            lhs = jnp.concatenate([HU[k, :, beta].reshape(512, UP_W) for k in range(2)], axis=1)
            term = jnp.dot(lhs, out_columns(0, s), preferred_element_type=F32)
            acc[s, block_at(beta)] = term.reshape(2, 2, 128, 256)
            return carry

        lax.fori_loop(0, 4 * N_OUT, tile, 0)

    near = [unit("up", k, 0) for k in range(2)]
    middle = [unit("up", k, 1) for k in range(2)]
    far = [unit("up", k, 2) for k in range(2)]
    whole = unit("up", 2)
    full, shared = unit("full", 3), unit("shared", 4)

    core_msgs[0].wait_recv()
    produce(near[0])
    combine(near[0])
    activate(near[0])
    produce(near[1])
    gather_forward()
    combine(near[1])
    gather_near()
    produce(middle[0])
    produce(middle[1])
    forward(near[0])
    combine(middle[0])
    activate(near[1])
    combine(middle[1])
    gather_far()
    produce(far[0])
    produce(far[1])
    forward(near[1])
    activate(middle[0])
    combine(far[0])
    activate(middle[1])
    combine(far[1])
    produce(whole)
    activate(far[0])
    activate(far[1])
    forward(middle[0])
    forward(middle[1])
    combine(whole)
    forward(far[0])
    forward(far[1])
    produce(full)
    activate(whole)
    combine(full)
    produce(shared)
    forward(whole)
    landed(near[0], middle[0], far[0])
    landed(near[1], middle[1], far[1])
    combine(shared)
    activate(full)
    second_product()
    activate(shared)
    forward(full)
    landed(whole)
    forward(shared)
    columns_ready(mine_w2, partner_w2, 1)
    landed(full)
    landed(shared)

    def out_core(s):
        columns = out_columns(512, s)

        def one(beta, carry):
            b = block_at(beta)
            lhs = jnp.concatenate([HU[2, :, beta].reshape(512, UP_W), HF[b], HS[b].reshape(512, HD)], axis=1)
            term = jnp.dot(lhs, columns, preferred_element_type=F32).reshape(2, 2, 128, 256)
            acc[s, b] += term
            OS[s, b] = acc[s, b, :, 1 - c].astype(BF16)
            return carry

        lax.fori_loop(0, 4, one, 0)
        return send(OS.at[s], OC.at[s], sib)

    def out_first(s, message):
        message.wait_recv()

        def one(d, carry):
            OC[s, d] = (OC[s, d].astype(F32) + acc[s, d, :, c]).astype(BF16)
            return carry

        lax.fori_loop(0, 4, one, 0)
        if s < 3:
            ring = Ring(
                send, y, yr, yl, lambda i, half: OC.at[s, i, half], Y0A.at[s, 0], Y0A.at[s, 1],
                [Y0B.at[s, 0, half] for half in range(2)], [Y0B.at[s, 1, half] for half in range(2)],
            )
        else:
            ring = Ring(
                send, z, zr, zlft,
                lambda i, half: OC.at[s, pl.ds(2 * half, 2), i % 2, :, part(128, i // 2)],
                Z1A.at[s - 3, 0], Z1A.at[s - 3, 1],
                [Z1B.at[s - 3, 0, half] for half in range(2)], [Z1B.at[s - 3, 1, half] for half in range(2)],
            )
        ring.first()
        ring.second()
        return ring

    def out_second(s, before):
        before.arrive()
        if s < 3:
            for half in range(2):
                Z0P[s, half] = before.total(half).astype(BF16)
            ring = Ring(
                send, z, zr, zlft,
                lambda i, half: Z0P.at[s, i % 2, pl.ds(64 * half, 64), part(128, i // 2)],
                Z0A.at[s, 0], Z0A.at[s, 1],
                [Z0B.at[s, 0, half] for half in range(2)], [Z0B.at[s, 1, half] for half in range(2)],
            )
        else:
            j = s - 3
            for half in range(2):
                Y1P[j, 2 * half : 2 * half + 2] = before.total(half).astype(BF16)
            ring = Ring(
                send, y, yr, yl, lambda i, half: Y1P.at[j, i, pl.ds(64 * half, 64)],
                Y1A.at[j, 0], Y1A.at[j, 1],
                [Y1B.at[j, 0, half] for half in range(2)], [Y1B.at[j, 1, half] for half in range(2)],
            )
        ring.first()
        ring.second()
        return ring

    def out_last(s, ring):
        ring.arrive()
        for half in range(2):
            rows, columns = slice(64 * half, 64 * half + 64), slice(128 * s, 128 * s + 128)
            out[rows, columns] = (tok[rows, columns].astype(F32) + ring.total(half)).astype(BF16)

    sequence = (0, 3, 1, 4, 2, 5)
    core, one, two = {}, {}, {}
    for t in range(N_OUT + 5):
        if t < N_OUT:
            core[t] = out_core(sequence[t])
        if 0 <= t - 1 < N_OUT:
            one[t - 1] = out_first(sequence[t - 1], core[t - 1])
        if 0 <= t - 2 < N_OUT:
            one[t - 2].third()
        if 0 <= t - 3 < N_OUT:
            two[t - 3] = out_second(sequence[t - 3], one[t - 3])
        if 0 <= t - 4 < N_OUT:
            two[t - 4].third()
        if 0 <= t - 5 < N_OUT:
            out_last(sequence[t - 5], two[t - 5])
    for copy in sent:
        copy.wait_send()


def vm(*shape, dtype=BF16):
    return pltpu.VMEM(shape, dtype)


def body(tokens, ln_gain, w_qkv, w_up, w_out, w_down):
    scratch = [
        vm(4, 2, 2, 128, 1536), vm(1536, 384), vm(1536, 384), vm(N_UP, 1536, UP_W),
        vm(1024, 1536),
        vm(4, 512, 384), vm(4, 256, 384), vm(N_UP, 4, 4, 128, UP_W),
        vm(2, 256, 384), vm(2, 128, 384), vm(N_UP, 2, 2, 128, UP_W),
        vm(2, 512, 384), vm(2, 256, 384), vm(N_UP, 2, 4, 128, UP_W),
        vm(4, 512, 128), vm(4, 2, 256, 128), vm(N_UP, 4, 4, 128, UP_W),
        vm(N_OUT, 4, 2, 2, 128, 256, dtype=F32), vm(N_OUT, 4, 2, 128, 256), vm(N_OUT, 4, 2, 128, 256),
        vm(3, 2, 128, 256), vm(3, 2, 2, 128, 256), vm(3, 2, 128, 256), vm(3, 2, 64, 128), vm(3, 2, 2, 64, 128),
        vm(3, 2, 2, 128, 128), vm(3, 2, 2, 2, 128, 128), vm(3, 4, 128, 128), vm(3, 2, 64, 128), vm(3, 2, 2, 64, 128),
        vm(8, 16, 128, dtype=F32),
        pltpu.SemaphoreType.DMA((N_MSG,)), pltpu.SemaphoreType.DMA((N_MSG,)), pltpu.SemaphoreType.DMA((N_LOC,)),
    ]
    vmem, anywhere = pl.BlockSpec(memory_space=pltpu.VMEM), pl.BlockSpec(memory_space=pl.ANY)
    return pl.pallas_call(
        kernel,
        out_shape=jax.ShapeDtypeStruct((128, KB), BF16),
        in_specs=[vmem, vmem, anywhere, anywhere, anywhere, anywhere],
        out_specs=vmem,
        scratch_shapes=scratch,
        compiler_params=pltpu.CompilerParams(
            collective_id=0, has_side_effects=True, vmem_limit_bytes=62 << 20
        ),
        name="layer",
    )(tokens, ln_gain, jnp.transpose(w_qkv, (1, 0, 2)), w_up, w_out, w_down)


def solution(mesh):
    return jax.shard_map(
        body,
        mesh=mesh,
        in_specs=(
            P("col", "row"),
            P("row"),
            P("row", None, "col"),
            P("row", "col"),
            P("col", "row"),
            P("col", "row"),
        ),
        out_specs=P("col", "row"),
        check_vma=False,
    )
```

```python
import jax
import jax.numpy as jnp
from jax import lax
from jax.experimental import pallas as pl
from jax.experimental.pallas import tpu as pltpu
from jax.sharding import PartitionSpec as P

D = 6144
HD = 128
KB = 768
PATCH = 256
EPS = 1e-06
F32 = jnp.float32
BF16 = jnp.bfloat16
MESH = pl.DeviceIdType.MESH
N_UP = 3
UP_W = 256
N_MSG = 256
N_LOC = 24


def head_norm(v):
    average = jnp.mean(v, axis=-1, keepdims=True)
    square = jnp.mean(v * v, axis=-1, keepdims=True)
    return ((v - average) * lax.rsqrt(square - average * average + EPS)).astype(BF16)


def attend(qkv):
    q = head_norm(qkv[:, 0:HD])
    k = head_norm(qkv[:, HD : 2 * HD])
    v = qkv[:, 2 * HD : 3 * HD].astype(BF16)
    scores = lax.dot_general(q, k, (((1,), (1,)), ((), ())), preferred_element_type=F32) * HD ** (-0.5)
    weights = jnp.exp(scores)
    probabilities = (weights / jnp.sum(weights, axis=-1, keepdims=True)).astype(BF16)
    return jnp.dot(probabilities, v, preferred_element_type=F32).astype(BF16)


class Ring:
    def __init__(self, send, pos, right, left, piece, a_left, a_right, b_left, b_right):
        self.send, self.right, self.left, self.piece = send, right, left, piece
        self.pos = pos
        self.plus, self.minus, self.anti = (pos + 1) % 4, (pos + 3) % 4, (pos + 2) % 4
        self.a_left, self.a_right, self.b_left, self.b_right = a_left, a_right, b_left, b_right

    def first(self):
        self.ma_r = self.send(self.piece(self.anti, 0), self.a_left, self.right)
        self.ma_l = self.send(self.piece(self.anti, 1), self.a_right, self.left)

    def second(self):
        self.mb_r1 = self.send(self.piece(self.plus, 1), self.b_left[1], self.right)
        self.mb_l0 = self.send(self.piece(self.minus, 0), self.b_right[0], self.left)

    def third(self):
        self.ma_r.wait_recv()
        mine = self.piece(self.plus, 0)
        mine[...] = (mine[...].astype(F32) + self.a_left[...].astype(F32)).astype(BF16)
        self.mb_r0 = self.send(mine, self.b_left[0], self.right)
        self.ma_l.wait_recv()
        mine = self.piece(self.minus, 1)
        mine[...] = (mine[...].astype(F32) + self.a_right[...].astype(F32)).astype(BF16)
        self.mb_l1 = self.send(mine, self.b_right[1], self.left)

    def arrive(self):
        for message in (self.mb_r1, self.mb_l0, self.mb_r0, self.mb_l1):
            message.wait_recv()

    def total(self, half):
        return (
            self.piece(self.pos, half)[...].astype(F32)
            + self.b_left[half][...].astype(F32)
            + self.b_right[half][...].astype(F32)
        )


N_OUT = 6
GROUPS = ((0, 1), (1, 2), (3, 1))
BLOCK_OF = (0, 1, 3, 2)


def kernel(
    tok, gain, wq, wu, wo, wd, out,
    X, W1F, W1S, W1U, W2,
    PF, PS, PU, AF, AS, AU, BF, BS, BU, HF, HS, HU,
    acc, OS, OC, Y0A, Y0B, Z0P, Z0A, Z0B, Z1A, Z1B, Z2A, Z2B, Y1P, Y1A, Y1B,
    stats, send_sem, recv_sem, loc_sem,
):
    row, col = lax.axis_index("row"), lax.axis_index("col")
    x, zh = row // 2, row % 2
    y, zl, c = col // 4, (col // 2) % 2, col % 2
    z = zh * 2 + zl

    def dev(x_, y_, z_, c_):
        return (x_ * 2 + z_ // 2, y_ * 4 + (z_ % 2) * 2 + c_)

    xr, xl = dev((x + 1) % 4, y, z, c), dev((x + 3) % 4, y, z, c)
    yr, yl = dev(x, (y + 1) % 4, z, c), dev(x, (y + 3) % 4, z, c)
    zr, zlft = dev(x, y, (z + 1) % 4, c), dev(x, y, (z + 3) % 4, c)
    zp = dev(x, y, (z + 2) % 4, c)
    sib = dev(x, y, z, 1 - c)
    zo = 1 - zh

    barrier = pltpu.get_barrier_semaphore()
    row_others = [(lax.rem(row + i, 8), col) for i in range(1, 8)]
    everyone = row_others + [yr, yl, zr, zlft, sib]
    for who in everyone:
        pl.semaphore_signal(barrier, inc=1, device_id=who, device_id_type=MESH)

    used = [0, 0]
    sent = []

    def send(src, dst, who):
        i = used[0]
        used[0] += 1
        copy = pltpu.make_async_remote_copy(
            src_ref=src, dst_ref=dst, send_sem=send_sem.at[i], recv_sem=recv_sem.at[i],
            device_id=who, device_id_type=MESH,
        )
        copy.start()
        sent.append(copy)
        return copy

    def local(src, dst):
        i = used[1]
        used[1] += 1
        copy = pltpu.make_async_copy(src, dst, loc_sem.at[i])
        copy.start()
        return copy

    def part(n, where):
        return pl.ds(pl.multiple_of(where * n, n), n)

    for d in range(4):
        HS[d, zo] = jnp.zeros((PATCH, HD), BF16)

    own_k = part(KB, zh)

    values = tok[...].astype(F32)
    sums = [jnp.sum(values, axis=-1, keepdims=True), jnp.sum(values * values, axis=-1, keepdims=True)]
    for i, s in enumerate(sums):
        stats[0, 8 * i : 8 * i + 8] = jnp.transpose(jnp.broadcast_to(s, (128, 128)))[0:8]
    pl.semaphore_wait(barrier, len(everyone))
    moments = [send(stats.at[0], stats.at[i + 1], who) for i, who in enumerate(row_others)]

    def w1_full(who):
        return [(wq.at[j, :, part(HD, 2 * who)], W1F.at[own_k, pl.ds(j * HD, HD)]) for j in range(3)]

    w1_shared = [(wq.at[j, :, pl.ds(HD, HD)], W1S.at[own_k, pl.ds(j * HD, HD)]) for j in range(3)]

    def up_part(who, k):
        return pl.ds(pl.multiple_of(who * KB + k * UP_W, UP_W), UP_W)

    def w1_parts(who):
        parts = [[(wu.at[:, up_part(who, k)], W1U.at[k, own_k])] for k in range(N_UP)]
        return parts[:2] + [w1_full(who), w1_shared, parts[2]]

    def w2_parts(who):
        return [
            [(wd.at[pl.ds(pl.multiple_of(who * KB, KB), 512)], W2.at[pl.ds(0, 512), own_k])],
            [
                (wd.at[up_part(who, 2)], W2.at[pl.ds(512, UP_W), own_k]),
                (wo.at[part(HD, 2 * who)], W2.at[pl.ds(768, HD), own_k]),
                (wo.at[pl.ds(HD, HD)], W2.at[pl.ds(896, HD), own_k]),
            ],
        ]

    partner_w1 = [[send(*p, zp) for p in ps] for ps in w1_parts(zo)[:1]]
    mine_w1 = [[local(*p) for p in ps] for ps in w1_parts(zh)]
    mine_w2 = [[local(*p) for p in ps] for ps in w2_parts(zh)]
    for m in moments:
        m.wait_recv()
    all_sums = jnp.sum(stats[...], axis=0) / D
    average, square = all_sums[0:1], all_sums[8:9]
    scale = lax.rsqrt(square - average * average + EPS)
    average = jnp.transpose(jnp.broadcast_to(average, (128, 128)))[:, 0:1]
    scale = jnp.transpose(jnp.broadcast_to(scale, (128, 128)))[:, 0:1]
    X[y, zl, c, :, own_k] = ((values - average) * scale * gain[...].reshape(1, KB)).astype(BF16)

    own = X.at[y, zl, c, :, own_k]
    z_msgs = {3: send(own, own, zr), 1: send(own, own, zlft), 2: send(own, own, zp)}
    partner_w1 += [[send(*p, zp) for p in ps] for ps in w1_parts(zo)[1:]]
    partner_w2 = [[send(*p, zp) for p in ps] for ps in w2_parts(zo)]

    def x_piece(y_, step):
        z_ = (z + step) % 4
        return X.at[y_, z_ % 2, c, :, part(KB, z_ // 2)]

    yp, ym, ya = (y + 1) % 4, (y + 3) % 4, (y + 2) % 4
    y_r, y_l, core_msgs, fwd = {}, {}, {}, []
    for step in (0, 3, 1, 2):
        if step:
            z_msgs[step].wait_recv()
        y_r[step] = send(x_piece(y, step), x_piece(y, step), yr)
        y_l[step] = send(x_piece(y, step), x_piece(y, step), yl)
    core_msgs[0] = send(X.at[y, :, c], X.at[y, :, c], sib)

    def gather_forward():
        for step in (0, 3):
            y_r[step].wait_recv()
            fwd.append(send(x_piece(ym, step), x_piece(ym, step), yr))
        for step in (1, 2):
            y_l[step].wait_recv()
            fwd.append(send(x_piece(yp, step), x_piece(yp, step), yl))

    def gather_near():
        for step in (1, 2):
            y_r[step].wait_recv()
        core_msgs[2] = send(X.at[ym, :, c], X.at[ym, :, c], sib)
        for step in (0, 3):
            y_l[step].wait_recv()
        core_msgs[1] = send(X.at[yp, :, c], X.at[yp, :, c], sib)
        for i in (2, 1):
            core_msgs[i].wait_recv()

    def gather_far():
        for m in fwd:
            m.wait_recv()
        core_msgs[3] = send(X.at[ya, :, c], X.at[ya, :, c], sib)
        core_msgs[3].wait_recv()

    def unit(kind, k, group=None):
        if kind == "full":
            p, a, b, h = PF, AF, BF, HF
        elif kind == "shared":
            p, a, b, h = PS, AS, BS, HS
        else:
            p, a, b, h = PU.at[k], AU.at[k], BU.at[k], HU.at[k]
        rows = {"full": 256, "shared": 128}.get(kind)
        base = (zh,) if kind == "shared" else ()
        blocks = None

        def at(half=None):
            if rows:
                return () if half is None else (pl.ds(rows * half, rows),)
            if group is None:
                return () if half is None else (pl.ds(2 * half, 2),)
            if group == 1:
                return (pl.ds(1, 2),) if half is None else (1 + half,)
            return (blocks[0],) if half is None else (blocks[0], pl.ds(64 * half, 64))

        if kind == "up":
            blocks = {None: (0, 1, 2, 3), 0: (0,), 1: (1, 2), 2: (3,)}[group]
        if rows or group is None:
            a_l, a_r = a.at[0], a.at[1]
        elif group == 1:
            a_l, a_r = a.at[0, 1], a.at[1, 1]
        else:
            a_l, a_r = (a.at[side, 0, pl.ds(32 * group, 64)] for side in range(2))
        ring = Ring(
            send, x, xr, xl, lambda i, half: p.at[(i, *at(half))], a_l, a_r,
            [b.at[(0, *at(half))] for half in range(2)], [b.at[(1, *at(half))] for half in range(2)],
        )
        weights = 4 if kind == "up" and k == 2 else k
        return dict(kind=kind, k=k, w=weights, p=p, h=h, at=at, base=base, blocks=blocks, ring=ring)

    def columns_ready(parts, partner, k):
        for copy in parts[k]:
            copy.wait()
        for copy in partner[k]:
            copy.wait_recv()
        parts[k], partner[k] = [], []

    def produce(u):
        columns_ready(mine_w1, partner_w1, u["w"])
        kind, ring, p = u["kind"], u["ring"], u["p"]
        if kind == "up":
            w1, blocks = W1U.at[u["k"]], u["blocks"]

            def one(i, carry):
                beta = blocks[0] + i
                b = block_at(beta)
                term = jnp.dot(X[b].reshape(512, 2 * KB), w1[...], preferred_element_type=F32)
                p[:, beta] = term.reshape(4, 128, UP_W).astype(BF16)
                return carry

            lax.fori_loop(0, len(blocks), one, 0)
            ring.first()
            ring.second()
            return

        def place(d):
            if kind == "shared":
                lhs, w1 = X[d, zh].reshape(256, 2 * KB), W1S
            else:
                lhs, w1 = X[d].reshape(512, 2 * KB), W1F
            p[d] = jnp.dot(lhs, w1[...], preferred_element_type=F32).astype(BF16)

        place((x + 2) % 4)
        ring.first()

        def other(i, carry):
            place((x + 1 + 2 * i + i // 2 * 3) % 4)
            return carry

        lax.fori_loop(0, 3, other, 0)
        ring.second()

    def combine(u):
        u["ring"].third()

    def activate(u):
        kind, ring, h, at = u["kind"], u["ring"], u["h"], u["at"]
        ring.arrive()
        if kind == "up":
            for half in range(2):
                h[(x, *at(half))] = jax.nn.gelu(ring.total(half), approximate=True).astype(BF16)
        elif kind == "full":
            for half in range(2):
                h[(x, *at(half))] = attend(ring.total(half))
        else:
            h[x, zh] = attend(jnp.concatenate([ring.total(0), ring.total(1)], axis=0))
        mine = h.at[(x, *u["base"], *at())]
        u["g_r"] = send(mine, mine, xr)
        u["g_l"] = send(mine, mine, xl)

    def forward(u):
        h, at = u["h"], u["at"]
        u["g_r"].wait_recv()
        low = h.at[((x + 3) % 4, *u["base"], *at(0))]
        u["f_r"] = send(low, low, xr)
        u["g_l"].wait_recv()
        high = h.at[((x + 1) % 4, *u["base"], *at(1))]
        u["f_l"] = send(high, high, xl)

    def landed(*units):
        for u in units:
            u["f_r"].wait_recv()
            u["f_l"].wait_recv()

    def out_columns(first, s):
        rows = pl.ds(first, 512)
        left, right = part(128, s), pl.ds(pl.multiple_of(KB + s * 128, 128), 128)
        return jnp.concatenate([W2[rows, left], W2[rows, right]], axis=1)

    def block_at(beta):
        return (y + beta + beta // 2 - 2 * (beta // 3)) % 4

    def second_product():
        columns_ready(mine_w2, partner_w2, 0)

        def tile(i, carry):
            beta, s = i // N_OUT, i % N_OUT
            lhs = jnp.concatenate([HU[k, :, beta].reshape(512, UP_W) for k in range(2)], axis=1)
            term = jnp.dot(lhs, out_columns(0, s), preferred_element_type=F32)
            acc[s, beta] = term.reshape(2, 2, 128, 256)
            return carry

        lax.fori_loop(0, 4 * N_OUT, tile, 0)

    near = [unit("up", k, 0) for k in range(2)]
    middle = [unit("up", k, 1) for k in range(2)]
    far = [unit("up", k, 2) for k in range(2)]
    last = [unit("up", 2, group) for group in range(3)]
    full, shared = unit("full", 2), unit("shared", 3)

    core_msgs[0].wait_recv()
    produce(near[0])
    combine(near[0])
    activate(near[0])
    produce(near[1])
    gather_forward()
    combine(near[1])
    gather_near()
    produce(middle[0])
    produce(middle[1])
    forward(near[0])
    combine(middle[0])
    activate(near[1])
    combine(middle[1])
    gather_far()
    produce(far[0])
    produce(far[1])
    forward(near[1])
    activate(middle[0])
    combine(far[0])
    activate(middle[1])
    combine(far[1])
    produce(full)
    activate(far[0])
    activate(far[1])
    forward(middle[0])
    forward(middle[1])
    combine(full)
    forward(far[0])
    forward(far[1])
    produce(shared)
    activate(full)
    combine(shared)
    produce(last[2])
    produce(last[1])
    forward(full)
    activate(shared)
    combine(last[2])
    combine(last[1])
    produce(last[0])
    landed(near[0], middle[0], far[0])
    landed(near[1], middle[1], far[1])
    second_product()
    activate(last[2])
    combine(last[0])
    forward(shared)
    activate(last[1])
    forward(last[2])
    activate(last[0])
    forward(last[1])

    def out_core(group, path):
        beta0, n = GROUPS[group]

        def one(i, carry):
            beta, j = beta0 + i // 3, i % 3
            s, b = path * 3 + j, block_at(beta)
            lhs = jnp.concatenate([HU[2, :, beta].reshape(512, UP_W), HF[b], HS[b].reshape(512, HD)], axis=1)
            term = jnp.dot(lhs, out_columns(512, s), preferred_element_type=F32)
            acc[s, beta] += term.reshape(2, 2, 128, 256)
            OS[path, beta, j] = acc[s, beta, :, 1 - c].astype(BF16)
            return carry

        lax.fori_loop(0, 3 * n, one, 0)
        some = pl.ds(beta0, n)
        return send(OS.at[path, some], OC.at[path, some], sib)

    def out_add(group, path, message):
        beta0, n = GROUPS[group]
        message.wait_recv()

        def one(i, carry):
            beta, j = beta0 + i // 3, i % 3
            OC[path, beta, j] = (OC[path, beta, j].astype(F32) + acc[path * 3 + j, beta, :, c]).astype(BF16)
            return carry

        lax.fori_loop(0, 3 * n, one, 0)

    def z_ring(group):
        beta0, n = GROUPS[group]
        if n == 1:
            a, b = Z1A.at[beta0 // 3], Z1B.at[beta0 // 3]

            def piece(i, half):
                return OC.at[1, beta0, :, i % 2, pl.ds(64 * half, 64), part(128, i // 2)]
        else:
            a, b = Z2A, Z2B

            def piece(i, half):
                return OC.at[1, beta0 + half, :, i % 2, :, part(128, i // 2)]

        ring = Ring(
            send, z, zr, zlft, piece, a.at[0], a.at[1],
            [b.at[0, half] for half in range(2)], [b.at[1, half] for half in range(2)],
        )
        ring.first()
        ring.second()
        return ring

    def z_done(group, ring):
        beta0, n = GROUPS[group]
        ring.arrive()
        for half in range(2):
            if n == 1:
                Y1P[beta0, :, 64 * half : 64 * half + 64] = ring.total(half).astype(BF16)
            else:
                Y1P[beta0 + half] = ring.total(half).astype(BF16)

    y_first = Ring(
        send, 0, yr, yl, lambda i, half: OC.at[0, BLOCK_OF[i], :, half], Y0A.at[0], Y0A.at[1],
        [Y0B.at[0, half] for half in range(2)], [Y0B.at[1, half] for half in range(2)],
    )
    z_last = Ring(
        send, z, zr, zlft, lambda i, half: Z0P.at[i % 2, :, pl.ds(64 * half, 64), part(128, i // 2)],
        Z0A.at[0], Z0A.at[1],
        [Z0B.at[0, half] for half in range(2)], [Z0B.at[1, half] for half in range(2)],
    )
    y_last = Ring(
        send, 0, yr, yl, lambda i, half: Y1P.at[BLOCK_OF[i], :, pl.ds(64 * half, 64)], Y1A.at[0], Y1A.at[1],
        [Y1B.at[0, half] for half in range(2)], [Y1B.at[1, half] for half in range(2)],
    )

    def out_last(path, ring):
        ring.arrive()
        for half in range(2):
            total = ring.total(half)
            for j in range(3):
                rows, columns = slice(64 * half, 64 * half + 64), slice(128 * (3 * path + j), 128 * (3 * path + j + 1))
                out[rows, columns] = (tok[rows, columns].astype(F32) + total[j]).astype(BF16)

    columns_ready(mine_w2, partner_w2, 1)
    landed(full, shared)
    landed(last[2])
    far_core = [out_core(2, path) for path in range(2)]
    forward(last[0])
    out_add(2, 0, far_core[0])
    y_first.first()
    out_add(2, 1, far_core[1])
    far_z = z_ring(2)
    landed(last[1])
    mid_core = [out_core(1, path) for path in range(2)]
    far_z.third()
    out_add(1, 0, mid_core[0])
    y_first.second()
    out_add(1, 1, mid_core[1])
    mid_z = z_ring(1)
    y_first.third()
    z_done(2, far_z)
    y_last.first()
    landed(last[0])
    near_core = [out_core(0, path) for path in (1, 0)]
    mid_z.third()
    out_add(0, 1, near_core[0])
    near_z = z_ring(0)
    out_add(0, 0, near_core[1])
    z_done(1, mid_z)
    y_last.second()
    near_z.third()
    y_last.third()
    y_first.arrive()
    for half in range(2):
        Z0P[half] = y_first.total(half).astype(BF16)
    z_last.first()
    z_last.second()
    z_done(0, near_z)
    z_last.third()
    out_last(1, y_last)
    out_last(0, z_last)
    for copy in sent:
        copy.wait_send()


def vm(*shape, dtype=BF16):
    return pltpu.VMEM(shape, dtype)


def body(tokens, ln_gain, w_qkv, w_up, w_out, w_down):
    scratch = [
        vm(4, 2, 2, 128, 1536), vm(1536, 384), vm(1536, 384), vm(N_UP, 1536, UP_W),
        vm(1024, 1536),
        vm(4, 512, 384), vm(4, 256, 384), vm(N_UP, 4, 4, 128, UP_W),
        vm(2, 256, 384), vm(2, 128, 384), vm(N_UP, 2, 2, 128, UP_W),
        vm(2, 512, 384), vm(2, 256, 384), vm(N_UP, 2, 4, 128, UP_W),
        vm(4, 512, 128), vm(4, 2, 256, 128), vm(N_UP, 4, 4, 128, UP_W),
        vm(N_OUT, 4, 2, 2, 128, 256, dtype=F32), vm(2, 4, 3, 2, 128, 256), vm(2, 4, 3, 2, 128, 256),
        vm(2, 3, 128, 256), vm(2, 2, 3, 128, 256), vm(2, 3, 128, 256), vm(2, 3, 64, 128), vm(2, 2, 3, 64, 128),
        vm(2, 2, 3, 64, 128), vm(2, 2, 2, 3, 64, 128), vm(2, 3, 128, 128), vm(2, 2, 3, 128, 128),
        vm(4, 3, 128, 128), vm(2, 3, 64, 128), vm(2, 2, 3, 64, 128),
        vm(8, 16, 128, dtype=F32),
        pltpu.SemaphoreType.DMA((N_MSG,)), pltpu.SemaphoreType.DMA((N_MSG,)), pltpu.SemaphoreType.DMA((N_LOC,)),
    ]
    vmem, anywhere = pl.BlockSpec(memory_space=pltpu.VMEM), pl.BlockSpec(memory_space=pl.ANY)
    return pl.pallas_call(
        kernel,
        out_shape=jax.ShapeDtypeStruct((128, KB), BF16),
        in_specs=[vmem, vmem, anywhere, anywhere, anywhere, anywhere],
        out_specs=vmem,
        scratch_shapes=scratch,
        compiler_params=pltpu.CompilerParams(
            collective_id=0, has_side_effects=True, vmem_limit_bytes=62 << 20
        ),
        name="layer",
    )(tokens, ln_gain, jnp.transpose(w_qkv, (1, 0, 2)), w_up, w_out, w_down)


def solution(mesh):
    return jax.shard_map(
        body,
        mesh=mesh,
        in_specs=(
            P("col", "row"),
            P("row"),
            P("row", None, "col"),
            P("row", "col"),
            P("col", "row"),
            P("col", "row"),
        ),
        out_specs=P("col", "row"),
        check_vma=False,
    )
```

```python
import jax
import jax.numpy as jnp
from jax import lax
from jax.experimental import pallas as pl
from jax.experimental.pallas import tpu as pltpu
from jax.sharding import PartitionSpec as P

D = 6144
HD = 128
KB = 768
PATCH = 256
EPS = 1e-06
F32 = jnp.float32
BF16 = jnp.bfloat16
MESH = pl.DeviceIdType.MESH
N_UP = 3
UP_W = 256
N_MSG = 256
N_LOC = 40


def head_norm(v):
    average = jnp.mean(v, axis=-1, keepdims=True)
    square = jnp.mean(v * v, axis=-1, keepdims=True)
    return ((v - average) * lax.rsqrt(square - average * average + EPS)).astype(BF16)


def attend(qkv):
    q = head_norm(qkv[:, 0:HD])
    k = head_norm(qkv[:, HD : 2 * HD])
    v = qkv[:, 2 * HD : 3 * HD].astype(BF16)
    scores = lax.dot_general(q, k, (((1,), (1,)), ((), ())), preferred_element_type=F32) * HD ** (-0.5)
    weights = jnp.exp(scores)
    probabilities = (weights / jnp.sum(weights, axis=-1, keepdims=True)).astype(BF16)
    return jnp.dot(probabilities, v, preferred_element_type=F32).astype(BF16)


class Ring:
    def __init__(self, send, pos, right, left, piece, a_left, a_right, b_left, b_right):
        self.send, self.right, self.left, self.piece = send, right, left, piece
        self.pos = pos
        self.plus, self.minus, self.anti = (pos + 1) % 4, (pos + 3) % 4, (pos + 2) % 4
        self.a_left, self.a_right, self.b_left, self.b_right = a_left, a_right, b_left, b_right

    def first(self):
        self.ma_r = self.send(self.piece(self.anti, 0), self.a_left, self.right)
        self.ma_l = self.send(self.piece(self.anti, 1), self.a_right, self.left)

    def second(self):
        self.mb_r1 = self.send(self.piece(self.plus, 1), self.b_left[1], self.right)
        self.mb_l0 = self.send(self.piece(self.minus, 0), self.b_right[0], self.left)

    def third(self):
        self.ma_r.wait_recv()
        mine = self.piece(self.plus, 0)
        mine[...] = (mine[...].astype(F32) + self.a_left[...].astype(F32)).astype(BF16)
        self.mb_r0 = self.send(mine, self.b_left[0], self.right)
        self.ma_l.wait_recv()
        mine = self.piece(self.minus, 1)
        mine[...] = (mine[...].astype(F32) + self.a_right[...].astype(F32)).astype(BF16)
        self.mb_l1 = self.send(mine, self.b_right[1], self.left)

    def arrive(self):
        for message in (self.mb_r1, self.mb_l0, self.mb_r0, self.mb_l1):
            message.wait_recv()

    def total(self, half):
        return (
            self.piece(self.pos, half)[...].astype(F32)
            + self.b_left[half][...].astype(F32)
            + self.b_right[half][...].astype(F32)
        )


N_OUT = 6
GROUPS = ((0, 1), (1, 2), (3, 1))
BLOCK_OF = (0, 1, 3, 2)


def kernel(
    tok, gain, wq, wu, wo, wd, out,
    X, W1F, W1S, W1U, W2, TU, TF, TS, T2,
    PF, PS, PU, AF, AS, AU, BF, BS, BU, HF, HS, HU,
    acc, OS, OC, Y0A, Y0B, Z0P, Z0A, Z0B, Z1A, Z1B, Z2A, Z2B, Y1P, Y1A, Y1B,
    stats, send_sem, recv_sem, loc_sem,
):
    row, col = lax.axis_index("row"), lax.axis_index("col")
    x, zh = row // 2, row % 2
    y, zl, c = col // 4, (col // 2) % 2, col % 2
    z = zh * 2 + zl

    def dev(x_, y_, z_, c_):
        return (x_ * 2 + z_ // 2, y_ * 4 + (z_ % 2) * 2 + c_)

    xr, xl = dev((x + 1) % 4, y, z, c), dev((x + 3) % 4, y, z, c)
    yr, yl = dev(x, (y + 1) % 4, z, c), dev(x, (y + 3) % 4, z, c)
    zr, zlft = dev(x, y, (z + 1) % 4, c), dev(x, y, (z + 3) % 4, c)
    zp = dev(x, y, (z + 2) % 4, c)
    sib = dev(x, y, z, 1 - c)
    zo = 1 - zh

    barrier = pltpu.get_barrier_semaphore()
    row_others = [(lax.rem(row + i, 8), col) for i in range(1, 8)]
    everyone = row_others + [yr, yl, zr, zlft, sib]
    for who in everyone:
        pl.semaphore_signal(barrier, inc=1, device_id=who, device_id_type=MESH)

    used = [0, 0]
    sent = []

    def send(src, dst, who):
        i = used[0]
        used[0] += 1
        copy = pltpu.make_async_remote_copy(
            src_ref=src, dst_ref=dst, send_sem=send_sem.at[i], recv_sem=recv_sem.at[i],
            device_id=who, device_id_type=MESH,
        )
        copy.start()
        sent.append(copy)
        return copy

    def local(src, dst):
        i = used[1]
        used[1] += 1
        copy = pltpu.make_async_copy(src, dst, loc_sem.at[i])
        copy.start()
        return copy

    def part(n, where):
        return pl.ds(pl.multiple_of(where * n, n), n)

    for d in range(4):
        HS[d, zo] = jnp.zeros((PATCH, HD), BF16)

    own_k = part(KB, zh)

    def up_part(who, k):
        return pl.ds(pl.multiple_of(who * KB + k * UP_W, UP_W), UP_W)

    def w1_parts(who, u, f, s):
        parts = [[(wu.at[:, up_part(who, k)], u(k))] for k in range(N_UP)]
        heads = [(wq.at[j, :, part(HD, 2 * who)], f(pl.ds(j * HD, HD))) for j in range(3)]
        shared = [(wq.at[j, :, pl.ds(HD, HD)], s(pl.ds(j * HD, HD))) for j in range(3)]
        return parts[:2] + [heads, shared, parts[2]]

    def w2_parts(who, at):
        return [
            [(wd.at[pl.ds(pl.multiple_of(who * KB, KB), 512)], at(pl.ds(0, 512)))],
            [
                (wd.at[up_part(who, 2)], at(pl.ds(512, UP_W))),
                (wo.at[part(HD, 2 * who)], at(pl.ds(768, HD))),
                (wo.at[pl.ds(HD, HD)], at(pl.ds(896, HD))),
            ],
        ]

    staged = w1_parts(zo, lambda k: TU.at[k], lambda cols: TF.at[:, cols], lambda cols: TS.at[:, cols])
    staged = [[local(*p) for p in ps] for ps in staged + w2_parts(zo, lambda rows: T2.at[rows])]
    mine_w1 = w1_parts(
        zh, lambda k: W1U.at[k, own_k], lambda cols: W1F.at[own_k, cols], lambda cols: W1S.at[own_k, cols]
    )
    mine_w1 = [[local(*p) for p in ps] for ps in mine_w1]
    mine_w2 = [[local(*p) for p in ps] for ps in w2_parts(zh, lambda rows: W2.at[zh, rows])]

    values = tok[...].astype(F32)
    sums = [jnp.sum(values, axis=-1, keepdims=True), jnp.sum(values * values, axis=-1, keepdims=True)]
    for i, s in enumerate(sums):
        stats[0, 8 * i : 8 * i + 8] = jnp.transpose(jnp.broadcast_to(s, (128, 128)))[0:8]
    pl.semaphore_wait(barrier, len(everyone))
    moments = [send(stats.at[0], stats.at[i + 1], who) for i, who in enumerate(row_others)]

    partner_w1, partner_w2 = [], []
    to_partner = [
        (partner_w1, TU.at[0], W1U.at[0, own_k]), (partner_w1, TU.at[1], W1U.at[1, own_k]),
        (partner_w1, TF, W1F.at[own_k]), (partner_w1, TS, W1S.at[own_k]),
        (partner_w1, TU.at[2], W1U.at[2, own_k]),
        (partner_w2, T2.at[pl.ds(0, 512)], W2.at[zh, pl.ds(0, 512)]),
        (partner_w2, T2.at[pl.ds(512, 512)], W2.at[zh, pl.ds(512, 512)]),
    ]

    def next_weights(n=1):
        for _ in range(n):
            into, src, dst = to_partner.pop(0)
            for copy in staged[7 - len(to_partner) - 1]:
                copy.wait()
            into.append([send(src, dst, zp)])

    next_weights(1)
    for m in moments:
        m.wait_recv()
    all_sums = jnp.sum(stats[...], axis=0) / D
    average, square = all_sums[0:1], all_sums[8:9]
    scale = lax.rsqrt(square - average * average + EPS)
    average = jnp.transpose(jnp.broadcast_to(average, (128, 128)))[:, 0:1]
    scale = jnp.transpose(jnp.broadcast_to(scale, (128, 128)))[:, 0:1]
    X[y, zl, c, :, own_k] = ((values - average) * scale * gain[...].reshape(1, KB)).astype(BF16)

    own = X.at[y, zl, c, :, own_k]
    z_msgs = {3: send(own, own, zr), 1: send(own, own, zlft), 2: send(own, own, zp)}
    next_weights(1)

    def x_piece(y_, step):
        z_ = (z + step) % 4
        return X.at[y_, z_ % 2, c, :, part(KB, z_ // 2)]

    yp, ym, ya = (y + 1) % 4, (y + 3) % 4, (y + 2) % 4
    y_r, y_l, core_msgs, fwd = {}, {}, {}, []
    for step in (0, 3, 1, 2):
        if step:
            z_msgs[step].wait_recv()
        y_r[step] = send(x_piece(y, step), x_piece(y, step), yr)
        y_l[step] = send(x_piece(y, step), x_piece(y, step), yl)
    core_msgs[0] = send(X.at[y, :, c], X.at[y, :, c], sib)

    def gather_forward():
        for step in (0, 3):
            y_r[step].wait_recv()
            fwd.append(send(x_piece(ym, step), x_piece(ym, step), yr))
        for step in (1, 2):
            y_l[step].wait_recv()
            fwd.append(send(x_piece(yp, step), x_piece(yp, step), yl))

    def gather_near():
        for step in (1, 2):
            y_r[step].wait_recv()
        core_msgs[2] = send(X.at[ym, :, c], X.at[ym, :, c], sib)
        for step in (0, 3):
            y_l[step].wait_recv()
        core_msgs[1] = send(X.at[yp, :, c], X.at[yp, :, c], sib)
        for i in (2, 1):
            core_msgs[i].wait_recv()

    def gather_far():
        for m in fwd:
            m.wait_recv()
        core_msgs[3] = send(X.at[ya, :, c], X.at[ya, :, c], sib)
        core_msgs[3].wait_recv()

    def unit(kind, k, group=None):
        if kind == "full":
            p, a, b, h = PF, AF, BF, HF
        elif kind == "shared":
            p, a, b, h = PS, AS, BS, HS
        else:
            p, a, b, h = PU.at[k], AU.at[k], BU.at[k], HU.at[k]
        rows = {"full": 256, "shared": 128}.get(kind)
        base = (zh,) if kind == "shared" else ()
        blocks = None

        def at(half=None):
            if rows:
                return () if half is None else (pl.ds(rows * half, rows),)
            if group is None:
                return () if half is None else (pl.ds(2 * half, 2),)
            if group == 1:
                return (pl.ds(1, 2),) if half is None else (1 + half,)
            return (blocks[0],) if half is None else (blocks[0], pl.ds(64 * half, 64))

        if kind == "up":
            blocks = {None: (0, 1, 2, 3), 0: (0,), 1: (1, 2), 2: (3,)}[group]
        if rows or group is None:
            a_l, a_r = a.at[0], a.at[1]
        elif group == 1:
            a_l, a_r = a.at[0, 1], a.at[1, 1]
        else:
            a_l, a_r = (a.at[side, 0, pl.ds(32 * group, 64)] for side in range(2))
        ring = Ring(
            send, x, xr, xl, lambda i, half: p.at[(i, *at(half))], a_l, a_r,
            [b.at[(0, *at(half))] for half in range(2)], [b.at[(1, *at(half))] for half in range(2)],
        )
        weights = 4 if kind == "up" and k == 2 else k
        return dict(kind=kind, k=k, w=weights, p=p, h=h, at=at, base=base, blocks=blocks, ring=ring)

    def columns_ready(parts, partner, k):
        for copy in parts[k]:
            copy.wait()
        for copy in partner[k]:
            copy.wait_recv()
        parts[k], partner[k] = [], []

    def produce(u):
        columns_ready(mine_w1, partner_w1, u["w"])
        kind, ring, p = u["kind"], u["ring"], u["p"]
        if kind == "up":
            w1, blocks = W1U.at[u["k"]], u["blocks"]

            def one(i, carry):
                beta = blocks[0] + i
                b = block_at(beta)
                term = jnp.dot(X[b].reshape(512, 2 * KB), w1[...], preferred_element_type=F32)
                p[:, beta] = term.reshape(4, 128, UP_W).astype(BF16)
                return carry

            lax.fori_loop(0, len(blocks), one, 0)
            ring.first()
            ring.second()
            return

        def place(d):
            if kind == "shared":
                lhs, w1 = X[d, zh].reshape(256, 2 * KB), W1S
            else:
                lhs, w1 = X[d].reshape(512, 2 * KB), W1F
            p[d] = jnp.dot(lhs, w1[...], preferred_element_type=F32).astype(BF16)

        place((x + 2) % 4)
        ring.first()

        def other(i, carry):
            place((x + 1 + 2 * i + i // 2 * 3) % 4)
            return carry

        lax.fori_loop(0, 3, other, 0)
        ring.second()

    def combine(u):
        u["ring"].third()

    def activate(u):
        kind, ring, h, at = u["kind"], u["ring"], u["h"], u["at"]
        ring.arrive()
        if kind == "up":
            for half in range(2):
                h[(x, *at(half))] = jax.nn.gelu(ring.total(half), approximate=True).astype(BF16)
        elif kind == "full":
            for half in range(2):
                h[(x, *at(half))] = attend(ring.total(half))
        else:
            h[x, zh] = attend(jnp.concatenate([ring.total(0), ring.total(1)], axis=0))
        mine = h.at[(x, *u["base"], *at())]
        u["g_r"] = send(mine, mine, xr)
        u["g_l"] = send(mine, mine, xl)

    def forward(u):
        h, at = u["h"], u["at"]
        u["g_r"].wait_recv()
        low = h.at[((x + 3) % 4, *u["base"], *at(0))]
        u["f_r"] = send(low, low, xr)
        u["g_l"].wait_recv()
        high = h.at[((x + 1) % 4, *u["base"], *at(1))]
        u["f_l"] = send(high, high, xl)

    def landed(*units):
        for u in units:
            u["f_r"].wait_recv()
            u["f_l"].wait_recv()

    def out_columns(first, s):
        rows, columns = pl.ds(first, 512), part(128, s)
        return jnp.concatenate([W2[0, rows, columns], W2[1, rows, columns]], axis=1)

    def block_at(beta):
        return (y + beta + beta // 2 - 2 * (beta // 3)) % 4

    def second_product():
        columns_ready(mine_w2, partner_w2, 0)

        def tile(i, carry):
            beta, s = i // N_OUT, i % N_OUT
            lhs = jnp.concatenate([HU[k, :, beta].reshape(512, UP_W) for k in range(2)], axis=1)
            term = jnp.dot(lhs, out_columns(0, s), preferred_element_type=F32)
            acc[s, beta] = term.reshape(2, 2, 128, 256)
            return carry

        lax.fori_loop(0, 4 * N_OUT, tile, 0)

    near = [unit("up", k, 0) for k in range(2)]
    middle = [unit("up", k, 1) for k in range(2)]
    far = [unit("up", k, 2) for k in range(2)]
    last = [unit("up", 2, group) for group in range(3)]
    full, shared = unit("full", 2), unit("shared", 3)

    core_msgs[0].wait_recv()
    produce(near[0])
    next_weights(1)
    combine(near[0])
    gather_forward()
    activate(near[0])
    produce(near[1])
    combine(near[1])
    gather_near()
    next_weights(1)
    produce(middle[0])
    produce(middle[1])
    forward(near[0])
    combine(middle[0])
    activate(near[1])
    combine(middle[1])
    gather_far()
    next_weights(1)
    produce(far[0])
    produce(far[1])
    forward(near[1])
    activate(middle[0])
    combine(far[0])
    activate(middle[1])
    combine(far[1])
    produce(full)
    next_weights(1)
    activate(far[0])
    activate(far[1])
    forward(middle[0])
    forward(middle[1])
    combine(full)
    forward(far[0])
    forward(far[1])
    produce(shared)
    next_weights(1)
    activate(full)
    combine(shared)
    produce(last[2])
    produce(last[1])
    forward(full)
    activate(shared)
    combine(last[2])
    combine(last[1])
    produce(last[0])
    landed(near[0], middle[0], far[0])
    landed(near[1], middle[1], far[1])
    second_product()
    activate(last[2])
    combine(last[0])
    forward(shared)
    activate(last[1])
    forward(last[2])
    activate(last[0])
    forward(last[1])

    def out_core(group, path):
        beta0, n = GROUPS[group]

        def one(i, carry):
            beta, j = beta0 + i // 3, i % 3
            s, b = path * 3 + j, block_at(beta)
            lhs = jnp.concatenate([HU[2, :, beta].reshape(512, UP_W), HF[b], HS[b].reshape(512, HD)], axis=1)
            term = jnp.dot(lhs, out_columns(512, s), preferred_element_type=F32)
            acc[s, beta] += term.reshape(2, 2, 128, 256)
            OS[path, beta, j] = acc[s, beta, :, 1 - c].astype(BF16)
            return carry

        lax.fori_loop(0, 3 * n, one, 0)
        some = pl.ds(beta0, n)
        return send(OS.at[path, some], OC.at[path, some], sib)

    def out_add(group, path, message):
        beta0, n = GROUPS[group]
        message.wait_recv()

        def one(i, carry):
            beta, j = beta0 + i // 3, i % 3
            OC[path, beta, j] = (OC[path, beta, j].astype(F32) + acc[path * 3 + j, beta, :, c]).astype(BF16)
            return carry

        lax.fori_loop(0, 3 * n, one, 0)

    def z_ring(group):
        beta0, n = GROUPS[group]
        if n == 1:
            a, b = Z1A.at[beta0 // 3], Z1B.at[beta0 // 3]

            def piece(i, half):
                return OC.at[1, beta0, :, i % 2, pl.ds(64 * half, 64), part(128, i // 2)]
        else:
            a, b = Z2A, Z2B

            def piece(i, half):
                return OC.at[1, beta0 + half, :, i % 2, :, part(128, i // 2)]

        ring = Ring(
            send, z, zr, zlft, piece, a.at[0], a.at[1],
            [b.at[0, half] for half in range(2)], [b.at[1, half] for half in range(2)],
        )
        ring.first()
        ring.second()
        return ring

    def z_done(group, ring):
        beta0, n = GROUPS[group]
        ring.arrive()
        for half in range(2):
            if n == 1:
                Y1P[beta0, :, 64 * half : 64 * half + 64] = ring.total(half).astype(BF16)
            else:
                Y1P[beta0 + half] = ring.total(half).astype(BF16)

    y_first = Ring(
        send, 0, yr, yl, lambda i, half: OC.at[0, BLOCK_OF[i], :, half], Y0A.at[0], Y0A.at[1],
        [Y0B.at[0, half] for half in range(2)], [Y0B.at[1, half] for half in range(2)],
    )
    z_last = Ring(
        send, z, zr, zlft, lambda i, half: Z0P.at[i % 2, :, pl.ds(64 * half, 64), part(128, i // 2)],
        Z0A.at[0], Z0A.at[1],
        [Z0B.at[0, half] for half in range(2)], [Z0B.at[1, half] for half in range(2)],
    )
    y_last = Ring(
        send, 0, yr, yl, lambda i, half: Y1P.at[BLOCK_OF[i], :, pl.ds(64 * half, 64)], Y1A.at[0], Y1A.at[1],
        [Y1B.at[0, half] for half in range(2)], [Y1B.at[1, half] for half in range(2)],
    )

    def out_last(path, ring):
        ring.arrive()
        for half in range(2):
            total = ring.total(half)
            for j in range(3):
                rows, columns = slice(64 * half, 64 * half + 64), slice(128 * (3 * path + j), 128 * (3 * path + j + 1))
                out[rows, columns] = (tok[rows, columns].astype(F32) + total[j]).astype(BF16)

    columns_ready(mine_w2, partner_w2, 1)
    landed(full, shared)
    landed(last[2])
    far_core = [out_core(2, path) for path in range(2)]
    forward(last[0])
    out_add(2, 0, far_core[0])
    y_first.first()
    out_add(2, 1, far_core[1])
    far_z = z_ring(2)
    landed(last[1])
    mid_core = [out_core(1, path) for path in range(2)]
    far_z.third()
    out_add(1, 0, mid_core[0])
    y_first.second()
    out_add(1, 1, mid_core[1])
    mid_z = z_ring(1)
    y_first.third()
    z_done(2, far_z)
    y_last.first()
    landed(last[0])
    near_core = [out_core(0, path) for path in (1, 0)]
    mid_z.third()
    out_add(0, 1, near_core[0])
    near_z = z_ring(0)
    out_add(0, 0, near_core[1])
    z_done(1, mid_z)
    y_last.second()
    near_z.third()
    y_last.third()
    y_first.arrive()
    for half in range(2):
        Z0P[half] = y_first.total(half).astype(BF16)
    z_last.first()
    z_last.second()
    z_done(0, near_z)
    z_last.third()
    out_last(1, y_last)
    out_last(0, z_last)
    for copy in sent:
        copy.wait_send()


def vm(*shape, dtype=BF16):
    return pltpu.VMEM(shape, dtype)


def body(tokens, ln_gain, w_qkv, w_up, w_out, w_down):
    scratch = [
        vm(4, 2, 2, 128, 1536), vm(1536, 384), vm(1536, 384), vm(N_UP, 1536, UP_W),
        vm(2, 1024, KB),
        vm(N_UP, KB, UP_W), vm(KB, 384), vm(KB, 384), vm(1024, KB),
        vm(4, 512, 384), vm(4, 256, 384), vm(N_UP, 4, 4, 128, UP_W),
        vm(2, 256, 384), vm(2, 128, 384), vm(N_UP, 2, 2, 128, UP_W),
        vm(2, 512, 384), vm(2, 256, 384), vm(N_UP, 2, 4, 128, UP_W),
        vm(4, 512, 128), vm(4, 2, 256, 128), vm(N_UP, 4, 4, 128, UP_W),
        vm(N_OUT, 4, 2, 2, 128, 256, dtype=F32), vm(2, 4, 3, 2, 128, 256), vm(2, 4, 3, 2, 128, 256),
        vm(2, 3, 128, 256), vm(2, 2, 3, 128, 256), vm(2, 3, 128, 256), vm(2, 3, 64, 128), vm(2, 2, 3, 64, 128),
        vm(2, 2, 3, 64, 128), vm(2, 2, 2, 3, 64, 128), vm(2, 3, 128, 128), vm(2, 2, 3, 128, 128),
        vm(4, 3, 128, 128), vm(2, 3, 64, 128), vm(2, 2, 3, 64, 128),
        vm(8, 16, 128, dtype=F32),
        pltpu.SemaphoreType.DMA((N_MSG,)), pltpu.SemaphoreType.DMA((N_MSG,)), pltpu.SemaphoreType.DMA((N_LOC,)),
    ]
    vmem, anywhere = pl.BlockSpec(memory_space=pltpu.VMEM), pl.BlockSpec(memory_space=pl.ANY)
    return pl.pallas_call(
        kernel,
        out_shape=jax.ShapeDtypeStruct((128, KB), BF16),
        in_specs=[vmem, vmem, anywhere, anywhere, anywhere, anywhere],
        out_specs=vmem,
        scratch_shapes=scratch,
        compiler_params=pltpu.CompilerParams(
            collective_id=0, has_side_effects=True, vmem_limit_bytes=62 << 20
        ),
        name="layer",
    )(tokens, ln_gain, jnp.transpose(w_qkv, (1, 0, 2)), w_up, w_out, w_down)


def solution(mesh):
    return jax.shard_map(
        body,
        mesh=mesh,
        in_specs=(
            P("col", "row"),
            P("row"),
            P("row", None, "col"),
            P("row", "col"),
            P("col", "row"),
            P("col", "row"),
        ),
        out_specs=P("col", "row"),
        check_vma=False,
    )
```
